128 devices in a mesh: rows: 32 (over y, z, core), sub: 4 (over x).
Axes of the slice: x: 4, y: 4, z: 4, core: 2. Of those that a mesh axis runs over, the one named last changes fastest.
Arguments:
- vectors: bfloat16 [262144, 1024], P('rows'), may hold values from -6 to 6
- list_ids: int32 [262144], P('rows'), may hold values from 0 to 16383, as said below
- centroids: bfloat16 [16384, 1024], P(('rows', 'sub')), may hold values from -6 to 6
- rotation: bfloat16 [1024, 1024], P(None, 'sub'), may hold values from -0.1875 to 0.1875
- codes: int32 [64, 262144], P('sub', 'rows'), may hold values from 0 to 255, as said below
Outputs:
- codebooks: float32 [64, 256, 16], P('sub')
- cross_cov: float32 [1024, 1024], P('rows', 'sub')
The draws below stay inside these ranges and needn't reach their ends.
Inputs may be any that keep to these rules, and one draw needn't show every extreme that they name: `codes`: every code 0 to 255 appears in every sub-space. `list_ids`: the coarse lists are held in consecutive blocks of 16384 // (32 * 4) by the devices in the order of rows+sub; the vectors of one index of rows name exactly 32 distinct lists of every such block.
All inputs are finite; a program needn't handle non-finite values.
Results may differ from the reference program's by a relative error of at most 0.0047.
Values may be sent and summed in bfloat16 or wider, within the bound.
A program may use at most 192 MiB of HBM per device.

```python
import jax
import jax.numpy as jnp
from jax import lax

D = 1024
SUBS = 64
SUBW = 16
KS = 256
NLIST = 16384
ROWS_DEV = 8192
TOTAL = 262144
LIST_CAP = 32
N_ROWS = 32
DEVICES = 128


def draw_codes(key, part):
    key = jax.random.fold_in(key, 7)
    first_key, second_key = jax.random.split(key)
    random_codes = jax.random.randint(first_key, (SUBS, TOTAL), 0, KS).astype(jnp.int32)
    row_keys = jax.random.split(second_key, SUBS)
    covering = jax.vmap(lambda one_key: jax.random.permutation(one_key, KS))(row_keys).astype(jnp.int32)
    return jnp.concatenate([covering, random_codes[:, KS:]], axis=1)


def draw_list_ids(key, part):
    key = jax.random.fold_in(key, 11)
    own_count = NLIST // DEVICES
    pool_size = DEVICES * LIST_CAP
    rest_count = ROWS_DEV - pool_size
    pick_key, order_key, upper_key, index_key, shuffle_key = jax.random.split(key, 5)
    pick_keys = jax.random.split(pick_key, N_ROWS * DEVICES)
    offsets = jax.vmap(lambda one_key: jax.random.permutation(one_key, own_count)[:LIST_CAP])(pick_keys)
    offsets = offsets.astype(jnp.int32).reshape(N_ROWS, DEVICES, LIST_CAP)
    owners = jnp.arange(DEVICES, dtype=jnp.int32)[None, :, None] * own_count
    pool = (owners + offsets).reshape(N_ROWS, pool_size)
    order_keys = jax.random.split(order_key, N_ROWS)
    order = jax.vmap(lambda one_key: jax.random.permutation(one_key, pool_size))(order_keys).astype(jnp.int32)
    first = jnp.take_along_axis(pool, order, axis=1)
    upper = jax.random.randint(upper_key, (N_ROWS, rest_count), 1, pool_size + 1).astype(jnp.int32)
    index = jax.random.randint(index_key, (N_ROWS, rest_count), 0, upper).astype(jnp.int32)
    shuffle_keys = jax.random.split(shuffle_key, N_ROWS)
    shuffle = jax.vmap(lambda one_key: jax.random.permutation(one_key, pool_size))(shuffle_keys).astype(jnp.int32)
    index = jnp.take_along_axis(shuffle, index, axis=1)
    rest = jnp.take_along_axis(pool, index, axis=1)
    return jnp.concatenate([first, rest], axis=1).reshape(TOTAL).astype(jnp.int32)


def block_scale(own_key, shape, shards, least, high):
    loudness, own = 1.0, jax.random.fold_in(own_key, 6)
    for axis_at, blocks in shards:
        steps = jnp.exp(jax.random.uniform(jax.random.fold_in(own, axis_at), (blocks,), jnp.float32, least / len(shards), high / len(shards)))
        loudness = loudness * jnp.repeat(steps, shape[axis_at] // blocks).reshape([-1 if axis == axis_at else 1 for axis in range(len(shape))])
    return loudness


def centred(rng, extent, spread, reach, cuts=(), kind=jnp.bfloat16):
    loudness = block_scale(rng, extent, cuts, -0.22, 0.18) if cuts else 1.0
    entries = jax.random.normal(rng, extent, jnp.float32) * spread * loudness
    return jnp.minimum(jnp.maximum(entries, -reach), reach).astype(kind)


def setup_inputs(seed: int = 0) -> dict:
    streams_of = jax.random.split(jax.random.key(seed), 6)
    return {
        "vectors": centred(streams_of[0], (TOTAL, D), 1.0, 6.0, ((0, 32),)),
        "list_ids": draw_list_ids(jax.random.fold_in(streams_of[5], 71), 0),
        "centroids": centred(streams_of[2], (NLIST, D), 1.0, 6.0, ((0, 128),)),
        "rotation": centred(streams_of[3], (D, D), D ** -0.5, 0.1875, ((1, 4),)),
        "codes": draw_codes(jax.random.fold_in(streams_of[5], 71), 0),
    }


def per_space(codes_row, pieces):
    code_sums = jax.ops.segment_sum(pieces, codes_row, num_segments=KS)
    counts = jax.ops.segment_sum(jnp.ones(codes_row.shape, jnp.float32), codes_row, num_segments=KS)
    new_book = code_sums / counts[:, None]
    return new_book, jnp.take(new_book, codes_row, axis=0)


def reference(vectors, list_ids, centroids, rotation, codes):
    fetched = jnp.take(centroids, list_ids, axis=0)
    residual = (vectors.astype(jnp.float32) - fetched.astype(jnp.float32)).astype(jnp.bfloat16)
    rotated = jnp.dot(residual, rotation, preferred_element_type=jnp.float32).astype(jnp.bfloat16)
    pieces = rotated.astype(jnp.float32).reshape(TOTAL, SUBS, SUBW).transpose(1, 0, 2)
    codebooks, rebuilt = lax.map(lambda pair: per_space(pair[0], pair[1]), (codes, pieces))
    rebuilt = rebuilt.transpose(1, 0, 2).reshape(TOTAL, D).astype(jnp.bfloat16)
    cross_cov = jnp.dot(residual.T, rebuilt, preferred_element_type=jnp.float32) / KS
    return codebooks, cross_cov
```

```python
import jax
import jax.numpy as jnp
from jax import lax
from jax.experimental import pallas as pl
from jax.experimental.pallas import tpu as pltpu
from jax.sharding import PartitionSpec as P

KS = 256
MIB = 2**20
MESH = pl.DeviceIdType.MESH
ROWS, SUBS = 32, 4


def load_table(place, mine_hbm, other_hbm, tab, sem):
    half = mine_hbm.shape[0]
    first = pltpu.make_async_copy(mine_hbm, tab.at[pl.ds(place[1] * half, half)], sem.at[0])
    second = pltpu.make_async_copy(
        other_hbm, tab.at[pl.ds((1 - place[1]) * half, half)], sem.at[1]
    )
    first.start()
    second.start()
    first.wait()
    second.wait()


def gather_rows(ids, base, tab, got, unroll=32):
    def body(i, carry):
        at = [ids[base + i * unroll + j] for j in range(unroll)]
        rows = [tab[at[j]] for j in range(unroll)]
        for j in range(unroll):
            got[i * unroll + j] = rows[j]
        return carry

    lax.fori_loop(0, got.shape[0] // unroll, body, 0)


def sums_kernel(ids, place, vr, codes, mine_hbm, other_hbm, part, tab, got, acc, sem):
    step = pl.program_id(0)
    rows = got.shape[0]

    @pl.when(step == 0)
    def _():
        load_table(place, mine_hbm, other_hbm, tab, sem)
        acc[...] = jnp.zeros_like(acc)

    gather_rows(ids, step * rows, tab, got)
    fetched = got[...].reshape(rows, 256).astype(jnp.float32)
    rotated = vr[...] - fetched
    turned = [rotated[:, h * 128:(h + 1) * 128].T.astype(jnp.bfloat16) for h in range(2)]
    subs = codes.shape[0]
    high = lax.broadcasted_iota(jnp.int32, (64, rows), 0)
    low = lax.broadcasted_iota(jnp.int32, (4, rows), 0)
    for grp in range(subs // 4):
        a, b, n = [], [], []
        for m in range(4 * grp, 4 * grp + 4):
            code = codes[m:m + 1, :]
            a.append((high == (code & 63)).astype(jnp.bfloat16))
            mine = (low == (code >> 6)).astype(jnp.bfloat16)
            piece = turned[m // 8][(m % 8) * 16:(m % 8 + 1) * 16, :]
            for l in range(4):
                b.append(piece * mine[l:l + 1, :])
            n.append(mine)
        left = jnp.concatenate(b + n, axis=0)
        right = jnp.concatenate(a, axis=0)
        acc[grp] += lax.dot_general(
            left, right, (((1,), (1,)), ((), ())), preferred_element_type=jnp.float32
        )

    @pl.when(step == pl.num_programs(0) - 1)
    def _():
        lane = lax.broadcasted_iota(jnp.int32, (1, 128), 1)
        for grp in range(subs // 4):
            for pair in range(2):
                cols = slice(pair * 128, pair * 128 + 128)
                m = 2 * pair
                even = acc[grp, m * 64:(m + 1) * 64, cols]
                odd = acc[grp, (m + 1) * 64:(m + 2) * 64, cols]
                both = jnp.where(lane < 64, even, odd)
                even = acc[grp, 256 + m * 4:256 + m * 4 + 4, cols]
                odd = acc[grp, 256 + m * 4 + 4:256 + m * 4 + 8, cols]
                count = jnp.where(lane < 64, even, odd)
                for l in range(4):
                    at = (2 * grp + pair) * 4 + l
                    part[at, :16, :] = both[l * 16:(l + 1) * 16, :]
                    part[at, 16:, :] = jnp.broadcast_to(count[l:l + 1, :], (8, 128))


def sums_call(ids, place, vr, codes, mine, other):
    rows, width = vr.shape
    subs = codes.shape[0]
    lists = 2 * mine.shape[0]
    tile = 1024
    return pl.pallas_call(
        sums_kernel,
        out_shape=jax.ShapeDtypeStruct((ROWS, 24, 128), jnp.float32),
        grid_spec=pltpu.PrefetchScalarGridSpec(
            num_scalar_prefetch=2,
            grid=(rows // tile,),
            in_specs=[
                pl.BlockSpec((tile, width), lambda i, s, p: (i, 0)),
                pl.BlockSpec((subs, tile), lambda i, s, p: (0, i)),
                pl.BlockSpec(memory_space=pl.ANY),
                pl.BlockSpec(memory_space=pl.ANY),
            ],
            out_specs=pl.BlockSpec((ROWS, 24, 128), lambda i, s, p: (0, 0, 0)),
            scratch_shapes=[
                pltpu.VMEM((lists, 2, 128), jnp.bfloat16),
                pltpu.VMEM((tile, 2, 128), jnp.bfloat16),
                pltpu.VMEM((subs // 4, 272, 256), jnp.float32),
                pltpu.SemaphoreType.DMA((2,)),
            ],
        ),
        compiler_params=pltpu.CompilerParams(vmem_limit_bytes=40 * MIB),
        cost_estimate=pl.CostEstimate(flops=4 * 10**9, bytes_accessed=18 * 10**6, transcendentals=0),
        name="code_sums",
    )(ids, place, vr, codes, mine, other)


def books_kernel(part, books, every, got, chunk, rounded, ssem, rsem, tsem, bsem, xsem, ysem):
    row = lax.axis_index("rows")
    sub = lax.axis_index("sub")
    barrier = pltpu.get_barrier_semaphore()

    def greet(p, carry):
        pl.semaphore_signal(
            barrier, inc=1, device_id=(lax.rem(row + p, ROWS), sub), device_id_type=MESH
        )
        return carry

    lax.fori_loop(1, ROWS, greet, 0)
    for p in range(1, SUBS):
        pl.semaphore_signal(
            barrier, inc=1, device_id=(row, lax.rem(sub + p, SUBS)), device_id_type=MESH
        )
    pl.semaphore_wait(barrier, ROWS - 1 + SUBS - 1)

    def scatter(p):
        to = lax.rem(row + p, ROWS)
        return pltpu.make_async_remote_copy(
            src_ref=part.at[to], dst_ref=got.at[row], send_sem=ssem.at[p],
            recv_sem=rsem.at[row], device_id=(to, sub), device_id_type=MESH,
        )

    def arrival(p):
        source = lax.rem(row + p, ROWS)
        return pltpu.make_async_remote_copy(
            src_ref=part.at[source], dst_ref=got.at[source], send_sem=ssem.at[p],
            recv_sem=rsem.at[source], device_id=(source, sub), device_id_type=MESH,
        )

    lax.fori_loop(1, ROWS, lambda p, c: (scatter(p).start(), c)[1], 0)

    def add(p, total):
        arrival(p).wait_recv()
        return total + got[lax.rem(row + p, ROWS)]

    total = lax.fori_loop(1, ROWS, add, part[row])
    mean = total[:16, :] / total[16:17, :]
    chunk[...] = mean
    books[row] = mean

    def spread(p):
        return pltpu.make_async_remote_copy(
            src_ref=chunk, dst_ref=books.at[row], send_sem=tsem.at[p],
            recv_sem=bsem.at[row], device_id=(lax.rem(row + p, ROWS), sub), device_id_type=MESH,
        )

    def landed(p):
        source = lax.rem(row + p, ROWS)
        return pltpu.make_async_remote_copy(
            src_ref=chunk, dst_ref=books.at[source], send_sem=tsem.at[p],
            recv_sem=bsem.at[source], device_id=(source, sub), device_id_type=MESH,
        )

    lax.fori_loop(1, ROWS, lambda p, c: (spread(p).start(), c)[1], 0)
    lax.fori_loop(1, ROWS, lambda p, c: (landed(p).wait_recv(), c)[1], 0)
    rounded[...] = books[...].astype(jnp.bfloat16)
    every[sub] = rounded[...]

    def across(p):
        return pltpu.make_async_remote_copy(
            src_ref=rounded, dst_ref=every.at[sub], send_sem=xsem.at[p],
            recv_sem=ysem.at[sub], device_id=(row, lax.rem(sub + p, SUBS)), device_id_type=MESH,
        )

    def crossed(p):
        source = lax.rem(sub + p, SUBS)
        return pltpu.make_async_remote_copy(
            src_ref=rounded, dst_ref=every.at[source], send_sem=xsem.at[p],
            recv_sem=ysem.at[source], device_id=(row, source), device_id_type=MESH,
        )

    for p in range(1, SUBS):
        across(p).start()
    for p in range(1, SUBS):
        crossed(p).wait_recv()
        across(p).wait_send()

    def sent(p, carry):
        scatter(p).wait_send()
        spread(p).wait_send()
        return carry

    lax.fori_loop(1, ROWS, sent, 0)


def books_call(part):
    vmem = pl.BlockSpec(memory_space=pltpu.VMEM)
    return pl.pallas_call(
        books_kernel,
        out_shape=(
            jax.ShapeDtypeStruct((ROWS, 16, 128), jnp.float32),
            jax.ShapeDtypeStruct((SUBS, ROWS, 16, 128), jnp.bfloat16),
        ),
        in_specs=[vmem],
        out_specs=(vmem, vmem),
        scratch_shapes=[
            pltpu.VMEM((ROWS, 24, 128), jnp.float32),
            pltpu.VMEM((16, 128), jnp.float32),
            pltpu.VMEM((ROWS, 16, 128), jnp.bfloat16),
            pltpu.SemaphoreType.DMA((ROWS,)),
            pltpu.SemaphoreType.DMA((ROWS,)),
            pltpu.SemaphoreType.DMA((ROWS,)),
            pltpu.SemaphoreType.DMA((ROWS,)),
            pltpu.SemaphoreType.DMA((SUBS,)),
            pltpu.SemaphoreType.DMA((SUBS,)),
        ],
        compiler_params=pltpu.CompilerParams(collective_id=1, has_side_effects=True),
        name="books",
    )(part)


def cross_kernel(ids, place, v, codes, every, mine_hbm, other_hbm, out, tab, got, books, rebuilt, acc, sem):
    step = pl.program_id(0)
    rows = got.shape[0]
    groups = codes.shape[0]

    @pl.when(step == 0)
    def _():
        load_table(place, mine_hbm, other_hbm, tab, sem)
        acc[...] = jnp.zeros_like(acc)
        lane = lax.broadcasted_iota(jnp.int32, (1, 128), 1)

        def relay(q, carry):
            for half in range(2):
                low = every[q, 2 * half].astype(jnp.float32)
                up = every[q, 2 * half + 1].astype(jnp.float32)
                books[2 * q, half] = jnp.where(lane < 64, low, pltpu.roll(up, 64, 1))
                books[2 * q + 1, half] = jnp.where(lane < 64, pltpu.roll(low, 64, 1), up)
            return carry

        lax.fori_loop(0, every.shape[0], relay, 0)

    gather_rows(ids, step * rows, tab, got)
    fetched = got[...].reshape(rows, 256).astype(jnp.float32)
    residual = (v[...].astype(jnp.float32) - fetched).T.astype(jnp.bfloat16)

    def space(g, carry):
        for j in range(8):
            m = g * 8 + j
            table = [[books[m, h, d * 8:(d + 1) * 8, :] for d in range(2)] for h in range(2)]
            for t in range(rows // 128):
                cols = slice(t * 128, (t + 1) * 128)
                code = jnp.broadcast_to(codes[g, j:j + 1, cols], (8, 128))
                at = code & 127
                both = []
                for d in range(2):
                    lo = jnp.take_along_axis(table[0][d], at, axis=1)
                    hi = jnp.take_along_axis(table[1][d], at, axis=1)
                    both.append(jnp.where(code >= 128, hi, lo))
                rebuilt[pl.ds(pl.multiple_of(m * 16, 16), 16), cols] = jnp.concatenate(
                    both, axis=0
                ).astype(jnp.bfloat16)
        return carry

    lax.fori_loop(0, groups, space, 0)
    acc[...] += lax.dot_general(
        residual, rebuilt[...], (((1,), (1,)), ((), ())), preferred_element_type=jnp.float32
    )

    @pl.when(step == pl.num_programs(0) - 1)
    def _():
        for r in range(8):
            for s in range(SUBS):
                out[r, s] = (
                    acc[r * 32:(r + 1) * 32, s * 256:(s + 1) * 256] * (1.0 / KS)
                ).astype(jnp.bfloat16)


def cross_call(ids, place, vectors, codes, every, mine, other):
    rows = vectors.shape[0]
    groups = codes.shape[0]
    lists = 2 * mine.shape[0]
    tile = 1024
    return pl.pallas_call(
        cross_kernel,
        out_shape=jax.ShapeDtypeStruct((8, SUBS, 32, 256), jnp.bfloat16),
        grid_spec=pltpu.PrefetchScalarGridSpec(
            num_scalar_prefetch=2,
            grid=(rows // tile,),
            in_specs=[
                pl.BlockSpec((tile, 256), lambda i, s, p: (i, p[0])),
                pl.BlockSpec((groups, 8, tile), lambda i, s, p: (0, 0, i)),
                pl.BlockSpec((groups * 4, 4, 16, 128), lambda i, s, p: (0, 0, 0, 0)),
                pl.BlockSpec(memory_space=pl.ANY),
                pl.BlockSpec(memory_space=pl.ANY),
            ],
            out_specs=pl.BlockSpec((8, SUBS, 32, 256), lambda i, s, p: (0, 0, 0, 0)),
            scratch_shapes=[
                pltpu.VMEM((lists, 2, 128), jnp.bfloat16),
                pltpu.VMEM((tile, 2, 128), jnp.bfloat16),
                pltpu.VMEM((groups * 8, 2, 16, 128), jnp.float32),
                pltpu.VMEM((groups * 128, tile), jnp.bfloat16),
                pltpu.VMEM((256, 1024), jnp.float32),
                pltpu.SemaphoreType.DMA((2,)),
            ],
        ),
        compiler_params=pltpu.CompilerParams(vmem_limit_bytes=40 * MIB),
        cost_estimate=pl.CostEstimate(flops=5 * 10**9, bytes_accessed=18 * 10**6, transcendentals=0),
        name="cross",
    )(ids, place, vectors, codes, every, mine, other)


def spread_kernel(part, out, got, ssem, rsem):
    row = lax.axis_index("rows")
    sub = lax.axis_index("sub")
    block = row // 8
    own = (sub == block).astype(jnp.int32)
    barrier = pltpu.get_barrier_semaphore()

    def greet(p, carry):
        to = lax.rem(row + p, ROWS)

        @pl.when(jnp.logical_or(to != row, sub != block))
        def _():
            pl.semaphore_signal(barrier, inc=1, device_id=(to, block), device_id_type=MESH)

        return carry

    lax.fori_loop(0, ROWS, greet, 0)
    pl.semaphore_wait(barrier, ROWS - own)

    def copy(p):
        r = lax.rem(row + p // SUBS, 8)
        s = lax.rem(sub + p, SUBS)
        to = sub * 8 + r
        return to, s, r

    def send(p, carry):
        to, s, r = copy(p)
        here = jnp.logical_and(to == row, s == sub)

        @pl.when(here)
        def _():
            pltpu.make_async_copy(part.at[r, s], got.at[row], rsem.at[row]).start()

        @pl.when(jnp.logical_not(here))
        def _():
            pltpu.make_async_remote_copy(
                src_ref=part.at[r, s], dst_ref=got.at[row], send_sem=ssem.at[p],
                recv_sem=rsem.at[row], device_id=(to, s), device_id_type=MESH,
            ).start()

        return carry

    lax.fori_loop(0, ROWS, send, 0)

    def add(p, total):
        source = lax.rem(row + p, ROWS)
        pltpu.make_async_copy(part.at[0, 0], got.at[source], rsem.at[source]).wait()
        return total + got[source].astype(jnp.float32)

    out[...] = lax.fori_loop(0, ROWS, add, jnp.zeros(out.shape, jnp.float32))

    def sent(p, carry):
        to, s, r = copy(p)

        @pl.when(jnp.logical_or(to != row, s != sub))
        def _():
            pltpu.make_async_remote_copy(
                src_ref=part.at[r, s], dst_ref=got.at[row], send_sem=ssem.at[p],
                recv_sem=rsem.at[row], device_id=(to, s), device_id_type=MESH,
            ).wait_send()

        return carry

    lax.fori_loop(0, ROWS, sent, 0)


def spread_call(part):
    vmem = pl.BlockSpec(memory_space=pltpu.VMEM)
    return pl.pallas_call(
        spread_kernel,
        out_shape=jax.ShapeDtypeStruct((32, 256), jnp.float32),
        in_specs=[vmem],
        out_specs=vmem,
        scratch_shapes=[
            pltpu.VMEM((ROWS, 32, 256), jnp.bfloat16),
            pltpu.SemaphoreType.DMA((ROWS,)),
            pltpu.SemaphoreType.DMA((ROWS,)),
        ],
        compiler_params=pltpu.CompilerParams(collective_id=2, has_side_effects=True),
        name="cross_sum",
    )(part)


def around(x):
    sub = lax.axis_index("sub")
    parts = [x]
    for p in range(1, SUBS):
        parts.append(lax.ppermute(x, "sub", [((i + p) % SUBS, i) for i in range(SUBS)]))
    stacked = jnp.zeros((SUBS,) + x.shape, x.dtype)
    for p, part in enumerate(parts):
        stacked = lax.dynamic_update_index_in_dim(stacked, part, lax.rem(sub + p, SUBS), 0)
    return stacked


def fetch(block):
    cores = [[2 * i + c for i in range(ROWS // 2)] for c in range(2)]
    mine = lax.all_gather(block, "rows", axis=0, tiled=True, axis_index_groups=cores)
    other = lax.ppermute(mine, "rows", [(i, i ^ 1) for i in range(ROWS)])
    return mine, other


def local(vectors, list_ids, centroids, rotation, codes):
    row = lax.axis_index("rows")
    sub = lax.axis_index("sub")
    place = jnp.stack([sub, lax.rem(row, 2)]).astype(jnp.int32)
    owner = list_ids // 512
    ids = (owner % 2) * 8192 + (owner // 2) * 512 + list_ids % 512
    near = around(centroids).reshape(512, 1024)
    turned = jnp.dot(near, rotation, preferred_element_type=jnp.float32)
    turned = turned.astype(jnp.bfloat16).reshape(512, 2, 128)
    columns = lax.dynamic_slice_in_dim(near, sub * 256, 256, 1).reshape(512, 2, 128)
    turned_tables = fetch(turned)
    column_tables = fetch(columns)
    vr = jnp.dot(vectors, rotation, preferred_element_type=jnp.float32)
    spaces = around(codes.astype(jnp.bfloat16)).astype(jnp.int32).reshape(8, 8, -1)
    part = sums_call(ids, place, vr, codes, *turned_tables)
    books, every = books_call(part)
    every = every.reshape(32, 4, 16, 128)
    partial = cross_call(ids, place, vectors, spaces, every, *column_tables)
    cross_cov = spread_call(partial)
    codebooks = books.reshape(8, 4, 16, 2, 64).transpose(0, 3, 1, 4, 2).reshape(16, 256, 16)
    return codebooks, cross_cov


def solution(mesh):
    placed = (
        P("rows", None),
        P("rows"),
        P(("rows", "sub"), None),
        P(None, "sub"),
        P("sub", "rows"),
    )
    return jax.shard_map(
        local,
        mesh=mesh,
        in_specs=placed,
        out_specs=(P("sub", None, None), P("rows", "sub")),
        check_vma=False,
    )
```

```python
import jax
import jax.numpy as jnp
from jax import lax
from jax.experimental import pallas as pl
from jax.experimental.pallas import tpu as pltpu
from jax.sharding import PartitionSpec as P

KS = 256
MIB = 2**20
MESH = pl.DeviceIdType.MESH
ROWS, SUBS = 32, 4


def load_table(table_hbm, tab, sem):
    copy = pltpu.make_async_copy(table_hbm, tab, sem)
    copy.start()
    copy.wait()


def gather_rows(ids, base, tab, got, unroll=32):
    def body(i, carry):
        at = [ids[base + i * unroll + j] for j in range(unroll)]
        rows = [tab[at[j]] for j in range(unroll)]
        for j in range(unroll):
            got[i * unroll + j] = rows[j]
        return carry

    lax.fori_loop(0, got.shape[0] // unroll, body, 0)


def sums_kernel(ids, v, rot, codes, table_hbm, part, tab, got, acc, sem):
    step = pl.program_id(0)
    rows = got.shape[0]

    @pl.when(step == 0)
    def _():
        load_table(table_hbm, tab, sem)
        acc[...] = jnp.zeros_like(acc)

    gather_rows(ids, step * rows, tab, got)
    fetched = got[...].reshape(rows, 256).astype(jnp.float32)
    rotated = jnp.dot(v[...], rot[...], preferred_element_type=jnp.float32) - fetched
    turned = [rotated[:, h * 128:(h + 1) * 128].T.astype(jnp.bfloat16) for h in range(2)]
    subs = codes.shape[0]
    high = lax.broadcasted_iota(jnp.int32, (64, rows), 0)
    low = lax.broadcasted_iota(jnp.int32, (4, rows), 0)
    for grp in range(subs // 4):
        a, b, n = [], [], []
        for m in range(4 * grp, 4 * grp + 4):
            code = codes[m:m + 1, :]
            a.append((high == (code & 63)).astype(jnp.bfloat16))
            mine = (low == (code >> 6)).astype(jnp.bfloat16)
            piece = turned[m // 8][(m % 8) * 16:(m % 8 + 1) * 16, :]
            for l in range(4):
                b.append(piece * mine[l:l + 1, :])
            n.append(mine)
        left = jnp.concatenate(b + n, axis=0)
        right = jnp.concatenate(a, axis=0)
        acc[grp] += lax.dot_general(
            left, right, (((1,), (1,)), ((), ())), preferred_element_type=jnp.float32
        )

    @pl.when(step == pl.num_programs(0) - 1)
    def _():
        lane = lax.broadcasted_iota(jnp.int32, (1, 128), 1)
        for grp in range(subs // 4):
            for pair in range(2):
                cols = slice(pair * 128, pair * 128 + 128)
                m = 2 * pair
                even = acc[grp, m * 64:(m + 1) * 64, cols]
                odd = acc[grp, (m + 1) * 64:(m + 2) * 64, cols]
                both = jnp.where(lane < 64, even, odd)
                even = acc[grp, 256 + m * 4:256 + m * 4 + 4, cols]
                odd = acc[grp, 256 + m * 4 + 4:256 + m * 4 + 8, cols]
                count = jnp.where(lane < 64, even, odd)
                for l in range(4):
                    at = (2 * grp + pair) * 4 + l
                    part[at, :16, :] = both[l * 16:(l + 1) * 16, :]
                    part[at, 16:, :] = jnp.broadcast_to(count[l:l + 1, :], (8, 128))


def sums_call(ids, vectors, rotation, codes, table):
    rows, width = vectors.shape
    subs = codes.shape[0]
    lists = table.shape[0]
    tile = 1024
    return pl.pallas_call(
        sums_kernel,
        out_shape=jax.ShapeDtypeStruct((ROWS, 24, 128), jnp.float32),
        grid_spec=pltpu.PrefetchScalarGridSpec(
            num_scalar_prefetch=1,
            grid=(rows // tile,),
            in_specs=[
                pl.BlockSpec((tile, width), lambda i, s: (i, 0)),
                pl.BlockSpec(rotation.shape, lambda i, s: (0, 0)),
                pl.BlockSpec((subs, tile), lambda i, s: (0, i)),
                pl.BlockSpec(memory_space=pl.ANY),
            ],
            out_specs=pl.BlockSpec((ROWS, 24, 128), lambda i, s: (0, 0, 0)),
            scratch_shapes=[
                pltpu.VMEM((lists, 2, 128), jnp.bfloat16),
                pltpu.VMEM((tile, 2, 128), jnp.bfloat16),
                pltpu.VMEM((subs // 4, 272, 256), jnp.float32),
                pltpu.SemaphoreType.DMA,
            ],
        ),
        compiler_params=pltpu.CompilerParams(vmem_limit_bytes=40 * MIB),
        cost_estimate=pl.CostEstimate(flops=35 * 10**9, bytes_accessed=18 * 10**6, transcendentals=0),
        name="code_sums",
    )(ids, vectors, rotation, codes, table)


def books_kernel(part, books, every, got, chunk, rounded, ssem, rsem, tsem, bsem, xsem, ysem):
    row = lax.axis_index("rows")
    sub = lax.axis_index("sub")
    barrier = pltpu.get_barrier_semaphore()

    def greet(p, carry):
        pl.semaphore_signal(
            barrier, inc=1, device_id=(lax.rem(row + p, ROWS), sub), device_id_type=MESH
        )
        return carry

    lax.fori_loop(1, ROWS, greet, 0)
    for p in range(1, SUBS):
        pl.semaphore_signal(
            barrier, inc=1, device_id=(row, lax.rem(sub + p, SUBS)), device_id_type=MESH
        )
    pl.semaphore_wait(barrier, ROWS - 1 + SUBS - 1)

    def scatter(p):
        to = lax.rem(row + p, ROWS)
        return pltpu.make_async_remote_copy(
            src_ref=part.at[to], dst_ref=got.at[row], send_sem=ssem.at[p],
            recv_sem=rsem.at[row], device_id=(to, sub), device_id_type=MESH,
        )

    def arrival(p):
        source = lax.rem(row + p, ROWS)
        return pltpu.make_async_remote_copy(
            src_ref=part.at[source], dst_ref=got.at[source], send_sem=ssem.at[p],
            recv_sem=rsem.at[source], device_id=(source, sub), device_id_type=MESH,
        )

    lax.fori_loop(1, ROWS, lambda p, c: (scatter(p).start(), c)[1], 0)

    def add(p, total):
        arrival(p).wait_recv()
        return total + got[lax.rem(row + p, ROWS)]

    total = lax.fori_loop(1, ROWS, add, part[row])
    mean = total[:16, :] / total[16:17, :]
    chunk[...] = mean
    books[row] = mean

    def spread(p):
        return pltpu.make_async_remote_copy(
            src_ref=chunk, dst_ref=books.at[row], send_sem=tsem.at[p],
            recv_sem=bsem.at[row], device_id=(lax.rem(row + p, ROWS), sub), device_id_type=MESH,
        )

    def landed(p):
        source = lax.rem(row + p, ROWS)
        return pltpu.make_async_remote_copy(
            src_ref=chunk, dst_ref=books.at[source], send_sem=tsem.at[p],
            recv_sem=bsem.at[source], device_id=(source, sub), device_id_type=MESH,
        )

    lax.fori_loop(1, ROWS, lambda p, c: (spread(p).start(), c)[1], 0)
    lax.fori_loop(1, ROWS, lambda p, c: (landed(p).wait_recv(), c)[1], 0)
    rounded[...] = books[...].astype(jnp.bfloat16)
    every[sub] = rounded[...]

    def across(p):
        return pltpu.make_async_remote_copy(
            src_ref=rounded, dst_ref=every.at[sub], send_sem=xsem.at[p],
            recv_sem=ysem.at[sub], device_id=(row, lax.rem(sub + p, SUBS)), device_id_type=MESH,
        )

    def crossed(p):
        source = lax.rem(sub + p, SUBS)
        return pltpu.make_async_remote_copy(
            src_ref=rounded, dst_ref=every.at[source], send_sem=xsem.at[p],
            recv_sem=ysem.at[source], device_id=(row, source), device_id_type=MESH,
        )

    for p in range(1, SUBS):
        across(p).start()
    for p in range(1, SUBS):
        crossed(p).wait_recv()
        across(p).wait_send()

    def sent(p, carry):
        scatter(p).wait_send()
        spread(p).wait_send()
        return carry

    lax.fori_loop(1, ROWS, sent, 0)


def books_call(part):
    vmem = pl.BlockSpec(memory_space=pltpu.VMEM)
    return pl.pallas_call(
        books_kernel,
        out_shape=(
            jax.ShapeDtypeStruct((ROWS, 16, 128), jnp.float32),
            jax.ShapeDtypeStruct((SUBS, ROWS, 16, 128), jnp.bfloat16),
        ),
        in_specs=[vmem],
        out_specs=(vmem, vmem),
        scratch_shapes=[
            pltpu.VMEM((ROWS, 24, 128), jnp.float32),
            pltpu.VMEM((16, 128), jnp.float32),
            pltpu.VMEM((ROWS, 16, 128), jnp.bfloat16),
            pltpu.SemaphoreType.DMA((ROWS,)),
            pltpu.SemaphoreType.DMA((ROWS,)),
            pltpu.SemaphoreType.DMA((ROWS,)),
            pltpu.SemaphoreType.DMA((ROWS,)),
            pltpu.SemaphoreType.DMA((SUBS,)),
            pltpu.SemaphoreType.DMA((SUBS,)),
        ],
        compiler_params=pltpu.CompilerParams(collective_id=1, has_side_effects=True),
        cost_estimate=pl.CostEstimate(flops=20 * 10**9, bytes_accessed=10**6, transcendentals=0),
        name="books",
    )(part)


def cross_kernel(ids, place, v, codes, every, table_hbm, out, tab, got, books, rebuilt, acc, sem):
    step = pl.program_id(0)
    rows = got.shape[0]
    groups = codes.shape[0]

    @pl.when(step == 0)
    def _():
        load_table(table_hbm, tab, sem)
        acc[...] = jnp.zeros_like(acc)
        lane = lax.broadcasted_iota(jnp.int32, (1, 128), 1)

        def relay(q, carry):
            for half in range(2):
                low = every[q, 2 * half].astype(jnp.float32)
                up = every[q, 2 * half + 1].astype(jnp.float32)
                books[2 * q, half] = jnp.where(lane < 64, low, pltpu.roll(up, 64, 1))
                books[2 * q + 1, half] = jnp.where(lane < 64, pltpu.roll(low, 64, 1), up)
            return carry

        lax.fori_loop(0, every.shape[0], relay, 0)

    gather_rows(ids, step * rows, tab, got)
    fetched = got[...].reshape(rows, 256).astype(jnp.float32)
    residual = (v[...].astype(jnp.float32) - fetched).T.astype(jnp.bfloat16)

    def space(g, carry):
        for j in range(8):
            m = g * 8 + j
            table = [[books[m, h, d * 8:(d + 1) * 8, :] for d in range(2)] for h in range(2)]
            for t in range(rows // 128):
                cols = slice(t * 128, (t + 1) * 128)
                code = jnp.broadcast_to(codes[g, j:j + 1, cols], (8, 128))
                at = code & 127
                both = []
                for d in range(2):
                    lo = jnp.take_along_axis(table[0][d], at, axis=1)
                    hi = jnp.take_along_axis(table[1][d], at, axis=1)
                    both.append(jnp.where(code >= 128, hi, lo))
                rebuilt[pl.ds(pl.multiple_of(m * 16, 16), 16), cols] = jnp.concatenate(
                    both, axis=0
                ).astype(jnp.bfloat16)
        return carry

    lax.fori_loop(0, groups, space, 0)
    acc[...] += lax.dot_general(
        residual, rebuilt[...], (((1,), (1,)), ((), ())), preferred_element_type=jnp.float32
    )

    @pl.when(step == pl.num_programs(0) - 1)
    def _():
        for r in range(8):
            for s in range(SUBS):
                out[r, s] = (
                    acc[r * 32:(r + 1) * 32, s * 256:(s + 1) * 256] * (1.0 / KS)
                ).astype(jnp.bfloat16)


def cross_call(ids, place, vectors, codes, every, table):
    rows = vectors.shape[0]
    groups = codes.shape[0]
    lists = table.shape[0]
    tile = 1024
    return pl.pallas_call(
        cross_kernel,
        out_shape=jax.ShapeDtypeStruct((8, SUBS, 32, 256), jnp.bfloat16),
        grid_spec=pltpu.PrefetchScalarGridSpec(
            num_scalar_prefetch=2,
            grid=(rows // tile,),
            in_specs=[
                pl.BlockSpec((tile, 256), lambda i, s, p: (i, p[0])),
                pl.BlockSpec((groups, 8, tile), lambda i, s, p: (0, 0, i)),
                pl.BlockSpec((groups * 4, 4, 16, 128), lambda i, s, p: (0, 0, 0, 0)),
                pl.BlockSpec(memory_space=pl.ANY),
            ],
            out_specs=pl.BlockSpec((8, SUBS, 32, 256), lambda i, s, p: (0, 0, 0, 0)),
            scratch_shapes=[
                pltpu.VMEM((lists, 2, 128), jnp.bfloat16),
                pltpu.VMEM((tile, 2, 128), jnp.bfloat16),
                pltpu.VMEM((groups * 8, 2, 16, 128), jnp.float32),
                pltpu.VMEM((groups * 128, tile), jnp.bfloat16),
                pltpu.VMEM((256, 1024), jnp.float32),
                pltpu.SemaphoreType.DMA,
            ],
        ),
        compiler_params=pltpu.CompilerParams(vmem_limit_bytes=40 * MIB),
        cost_estimate=pl.CostEstimate(flops=50 * 10**9, bytes_accessed=18 * 10**6, transcendentals=0),
        name="cross",
    )(ids, place, vectors, codes, every, table)


def spread_kernel(part, out, got, ssem, rsem):
    row = lax.axis_index("rows")
    sub = lax.axis_index("sub")
    block = row // 8
    own = (sub == block).astype(jnp.int32)
    barrier = pltpu.get_barrier_semaphore()

    def greet(p, carry):
        to = lax.rem(row + p, ROWS)

        @pl.when(jnp.logical_or(to != row, sub != block))
        def _():
            pl.semaphore_signal(barrier, inc=1, device_id=(to, block), device_id_type=MESH)

        return carry

    lax.fori_loop(0, ROWS, greet, 0)
    pl.semaphore_wait(barrier, ROWS - own)

    def copy(p):
        r = lax.rem(row + p // SUBS, 8)
        s = lax.rem(sub + p, SUBS)
        to = sub * 8 + r
        return to, s, r

    def send(p, carry):
        to, s, r = copy(p)
        here = jnp.logical_and(to == row, s == sub)

        @pl.when(here)
        def _():
            pltpu.make_async_copy(part.at[r, s], got.at[row], rsem.at[row]).start()

        @pl.when(jnp.logical_not(here))
        def _():
            pltpu.make_async_remote_copy(
                src_ref=part.at[r, s], dst_ref=got.at[row], send_sem=ssem.at[p],
                recv_sem=rsem.at[row], device_id=(to, s), device_id_type=MESH,
            ).start()

        return carry

    lax.fori_loop(0, ROWS, send, 0)

    def add(p, total):
        source = lax.rem(row + p, ROWS)
        pltpu.make_async_copy(part.at[0, 0], got.at[source], rsem.at[source]).wait()
        return total + got[source].astype(jnp.float32)

    out[...] = lax.fori_loop(0, ROWS, add, jnp.zeros(out.shape, jnp.float32))

    def sent(p, carry):
        to, s, r = copy(p)

        @pl.when(jnp.logical_or(to != row, s != sub))
        def _():
            pltpu.make_async_remote_copy(
                src_ref=part.at[r, s], dst_ref=got.at[row], send_sem=ssem.at[p],
                recv_sem=rsem.at[row], device_id=(to, s), device_id_type=MESH,
            ).wait_send()

        return carry

    lax.fori_loop(0, ROWS, sent, 0)


def spread_call(part):
    vmem = pl.BlockSpec(memory_space=pltpu.VMEM)
    return pl.pallas_call(
        spread_kernel,
        out_shape=jax.ShapeDtypeStruct((32, 256), jnp.float32),
        in_specs=[vmem],
        out_specs=vmem,
        scratch_shapes=[
            pltpu.VMEM((ROWS, 32, 256), jnp.bfloat16),
            pltpu.SemaphoreType.DMA((ROWS,)),
            pltpu.SemaphoreType.DMA((ROWS,)),
        ],
        compiler_params=pltpu.CompilerParams(collective_id=2, has_side_effects=True),
        name="cross_sum",
    )(part)


def around(x):
    sub = lax.axis_index("sub")
    parts = [x]
    for p in range(1, SUBS):
        parts.append(lax.ppermute(x, "sub", [((i + p) % SUBS, i) for i in range(SUBS)]))
    stacked = jnp.zeros((SUBS,) + x.shape, x.dtype)
    for p, part in enumerate(parts):
        stacked = lax.dynamic_update_index_in_dim(stacked, part, lax.rem(sub + p, SUBS), 0)
    return stacked


ROUNDS = ((0, 1), (1, 3), (3, 4))


def table_kernel(c, rot, table, columns, near, stage, ssem, rsem, xssem, xrsem, lsem):
    row = lax.axis_index("rows")
    sub = lax.axis_index("sub")
    core = lax.rem(row, 2)
    z = lax.rem(row // 2, 4)
    y = row // 8

    def up(i):
        return lax.rem(i + 1, 4)

    def down(i):
        return lax.rem(i + 3, 4)

    def device(at_y, at_z):
        return ((at_y * 4 + at_z) * 2 + core, sub)

    beside = (row + 1 - 2 * core, sub)
    after = {0: (device(up(y), z), device(down(y), z)), 1: (device(y, up(z)), device(y, down(z)))}
    across = ((row, up(sub)), (row, down(sub)))

    barrier = pltpu.get_barrier_semaphore()
    for peer in after[0] + after[1] + across + (beside,):
        pl.semaphore_signal(barrier, inc=1, device_id=peer, device_id_type=MESH)
    pl.semaphore_wait(barrier, 7)

    def remote(src, dst, send, recv, to):
        return pltpu.make_async_remote_copy(
            src_ref=src, dst_ref=dst, send_sem=send, recv_sem=recv,
            device_id=to, device_id_type=MESH,
        )

    def exchange(k):
        if k < 2:
            return remote(c, near.at[1 - k], xssem.at[k], xrsem.at[k], across[k])
        half = pl.ds((k - 2) * 64, 64)
        return remote(near.at[3 - k, half], near.at[2, half], xssem.at[k], xrsem.at[k], across[k - 2])

    exchange(0).start()
    exchange(1).start()

    def project(q, block):
        value = jnp.dot(block, rot[...], preferred_element_type=jnp.float32)
        value = value.astype(jnp.bfloat16).reshape(2, 64, 2, 128)
        stage[q] = value

    def hop(rnd, h, phase, k):
        first, last = ROUNDS[rnd]
        qs = pl.ds(first, last - first)
        u, w = (y, z) if h == 0 else (z, y)
        to = after[h if phase == 0 else 1 - h][k % 2]
        at = ((rnd * 2 + h) * 2 + phase) * 4 + k
        mine = table.at[core, h]
        part = pl.ds(0, 32) if k == 2 else pl.ds(32, 32)
        if phase == 0:
            dst = mine.at[w, u, qs]
            if k < 2:
                src = stage.at[qs, h]
            else:
                src = dst = mine.at[w, down(u) if k == 2 else up(u), qs, part]
        elif k < 2:
            src = dst = mine.at[w, :, qs]
        else:
            src = dst = mine.at[down(w) if k == 2 else up(w), :, qs, part]
        return remote(src, dst, ssem.at[at], rsem.at[at], to)

    def keep(rnd, h):
        first, last = ROUNDS[rnd]
        qs = pl.ds(first, last - first)
        u, w = (y, z) if h == 0 else (z, y)
        return pltpu.make_async_copy(
            stage.at[qs, h], table.at[core, h, w, u, qs], lsem.at[rnd * 2 + h]
        )

    def over(rnd, h):
        first, last = ROUNDS[rnd]
        part = table.at[core, h, :, :, pl.ds(first, last - first)]
        at = 48 + rnd * 2 + h
        return remote(part, part, ssem.at[at], rsem.at[at], beside)

    def start(rnd, phase, forward):
        for k in (2, 3) if forward else (0, 1):
            for h in range(2):
                if forward:
                    hop(rnd, h, phase, k - 2).wait_recv()
                hop(rnd, h, phase, k).start()

    def arrived(rnd, phase):
        for h in range(2):
            for k in (2, 3):
                hop(rnd, h, phase, k).wait_recv()

    def begin(rnd):
        for h in range(2):
            keep(rnd, h).start()
        start(rnd, 0, False)

    def second(rnd):
        arrived(rnd, 0)
        for h in range(2):
            keep(rnd, h).wait()
        start(rnd, 1, False)

    def finish(rnd):
        arrived(rnd, 1)
        for h in range(2):
            over(rnd, h).start()

    project(0, c[...])
    begin(0)
    for k in range(2):
        exchange(k).wait_recv()
        exchange(k + 2).start()
    start(0, 0, True)
    project(1, near[0])
    project(2, near[1])
    begin(1)
    second(0)
    exchange(2).wait_recv()
    exchange(3).wait_recv()
    project(3, near[2])
    begin(2)
    start(1, 0, True)
    second(1)
    start(2, 0, True)
    second(2)
    start(0, 1, True)
    first_column = pl.multiple_of(sub * 256, 256)
    for q in range(4):
        block = c[:, pl.ds(first_column, 256)] if q == 0 else near[q - 1, :, pl.ds(first_column, 256)]
        columns[q] = block.reshape(128, 2, 128)
    finish(0)
    start(1, 1, True)
    finish(1)
    start(2, 1, True)
    finish(2)
    for rnd in range(3):
        for h in range(2):
            over(rnd, h).wait()
            for phase in range(2):
                for k in range(4):
                    hop(rnd, h, phase, k).wait_send()
    for k in range(4):
        exchange(k).wait_send()


def table_call(centroids, rotation):
    vmem = pl.BlockSpec(memory_space=pltpu.VMEM)
    dma = pltpu.SemaphoreType.DMA
    return pl.pallas_call(
        table_kernel,
        out_shape=(
            jax.ShapeDtypeStruct((2, 2, 4, 4, 4, 64, 2, 128), jnp.bfloat16),
            jax.ShapeDtypeStruct((4, 128, 2, 128), jnp.bfloat16),
        ),
        in_specs=[vmem, vmem],
        out_specs=(pl.BlockSpec(memory_space=pl.ANY), vmem),
        scratch_shapes=[
            pltpu.VMEM((3, 128, 1024), jnp.bfloat16),
            pltpu.VMEM((4, 2, 64, 2, 128), jnp.bfloat16),
            dma((54,)),
            dma((54,)),
            dma((4,)),
            dma((4,)),
            dma((6,)),
        ],
        compiler_params=pltpu.CompilerParams(collective_id=3, has_side_effects=True),
        cost_estimate=pl.CostEstimate(flops=10**9, bytes_accessed=10**8, transcendentals=0),
        name="table",
    )(centroids, rotation)


def local(vectors, list_ids, centroids, rotation, codes):
    row = lax.axis_index("rows")
    sub = lax.axis_index("sub")
    place = jnp.stack([sub, lax.rem(row, 2)]).astype(jnp.int32)
    table, columns = table_call(centroids, rotation)
    column_table = lax.all_gather(columns, "rows", axis=0, tiled=True)
    spaces = around(codes.astype(jnp.bfloat16)).astype(jnp.int32).reshape(8, 8, -1)
    owner, inner = list_ids // 128, list_ids % 128
    at_row, at_sub = owner // 4, owner % 4
    near = jnp.array([0, 1, 3, 2], jnp.int32)[(at_sub - sub + 4) % 4]
    at_y, at_z, at_core = at_row // 8, (at_row // 2) % 4, at_row % 2
    half = inner // 64
    block = jnp.where(half == 0, at_z * 4 + at_y, at_y * 4 + at_z)
    ids = (((at_core * 2 + half) * 16 + block) * 4 + near) * 64 + inner % 64
    column_ids = (at_row * 4 + near) * 128 + inner
    part = sums_call(ids, vectors, rotation, codes, table.reshape(-1, 2, 128))
    books, every = books_call(part)
    every = every.reshape(32, 4, 16, 128)
    partial = cross_call(column_ids, place, vectors, spaces, every, column_table.reshape(-1, 2, 128))
    cross_cov = spread_call(partial)
    codebooks = books.reshape(8, 4, 16, 2, 64).transpose(0, 3, 1, 4, 2).reshape(16, 256, 16)
    return codebooks, cross_cov


def solution(mesh):
    placed = (
        P("rows", None),
        P("rows"),
        P(("rows", "sub"), None),
        P(None, "sub"),
        P("sub", "rows"),
    )
    return jax.shard_map(
        local,
        mesh=mesh,
        in_specs=placed,
        out_specs=(P("sub", None, None), P("rows", "sub")),
        check_vma=False,
    )
```

```python
import jax
import jax.numpy as jnp
from jax import lax
from jax.experimental import pallas as pl
from jax.experimental.pallas import tpu as pltpu
from jax.sharding import PartitionSpec as P

KS = 256
MIB = 2**20
MESH = pl.DeviceIdType.MESH
ROWS, SUBS = 32, 4
TILE, TILES = 1024, 8
ROUNDS = ((0, 1), (1, 3), (3, 4))
F32, BF16, I32 = jnp.float32, jnp.bfloat16, jnp.int32
TABLE = (2, 2, 4, 4, 4, 64, 2, 128)


def nt(a, b):
    return lax.dot_general(a, b, (((1,), (1,)), ((), ())), preferred_element_type=F32)


def step_kernel(
    ids, v, c, rot, codes, means, cross,
    tab1, tab2, near, stage1, stage2, vbuf, vr, got, turned, acc, part, partgot,
    chunk, bchunk, rounded, every, books, every_codes, resid, vcol, total, piece, piecegot,
    vsem, xs, xr, l1, s1, r1, l2, s2, r2, cs, cr, ps, pr, ms, mr, bs, br, ys, yr, ws, wr, vcsem,
):
    row = lax.axis_index("rows")
    sub = lax.axis_index("sub")
    core = lax.rem(row, 2)
    z = lax.rem(row // 2, 4)
    y = row // 8
    block = row // 8
    own = (sub == block).astype(I32)

    def up(i):
        return lax.rem(i + 1, 4)

    def down(i):
        return lax.rem(i + 3, 4)

    def device(at_y, at_z):
        return ((at_y * 4 + at_z) * 2 + core, sub)

    beside = (row + 1 - 2 * core, sub)
    after = ((device(up(y), z), device(down(y), z)), (device(y, up(z)), device(y, down(z))))
    across = ((row, up(sub)), (row, down(sub)))

    barrier = pltpu.get_barrier_semaphore()

    def greet(p, carry):
        to = lax.rem(row + p, ROWS)

        @pl.when(p > 0)
        def _():
            pl.semaphore_signal(barrier, inc=1, device_id=(to, sub), device_id_type=MESH)

        @pl.when(jnp.logical_or(p > 0, sub != block))
        def _():
            pl.semaphore_signal(barrier, inc=1, device_id=(to, block), device_id_type=MESH)

        return carry

    lax.fori_loop(0, ROWS, greet, 0)
    for p in range(1, SUBS):
        to = (row, lax.rem(sub + p, SUBS))
        pl.semaphore_signal(barrier, inc=1, device_id=to, device_id_type=MESH)

    def remote(src, dst, send, recv, to):
        return pltpu.make_async_remote_copy(
            src_ref=src, dst_ref=dst, send_sem=send, recv_sem=recv,
            device_id=to, device_id_type=MESH,
        )

    def v_copy(i):
        return pltpu.make_async_copy(
            v.at[pl.ds(i * TILE, TILE)], vbuf.at[lax.rem(i, 2)], vsem.at[lax.rem(i, 2)]
        )

    def turn_rows(first, last):
        def body(i, carry):
            v_copy(i).wait()

            @pl.when(i + 1 < TILES)
            def _():
                v_copy(i + 1).start()

            for h in range(2):
                value = jnp.dot(
                    vbuf[lax.rem(i, 2), h * 512:(h + 1) * 512, :], rot[...],
                    preferred_element_type=F32,
                )
                vr[pl.ds(pl.multiple_of(i * TILE + h * 512, 512), 512), :] = value
            return carry

        lax.fori_loop(first, last, body, 0)

    v_copy(0).start()
    turn_rows(0, 2)
    pl.semaphore_wait(barrier, 2 * ROWS + SUBS - 2 - own)

    def exchange(k):
        if k < 2:
            return remote(c, near.at[1 - k], xs.at[k], xr.at[k], across[k])
        half = pl.ds((k - 2) * 64, 64)
        return remote(near.at[3 - k, half], near.at[2, half], xs.at[k], xr.at[k], across[k - 2])

    class Gather:
        def __init__(self, table, stage, rounds, lsem, ssem, rsem):
            self.table, self.stage, self.rounds = table, stage, rounds
            self.lsem, self.ssem, self.rsem = lsem, ssem, rsem

        def hop(self, rnd, h, phase, k):
            first, last = self.rounds[rnd]
            qs = pl.ds(first, last - first)
            u, w = (y, z) if h == 0 else (z, y)
            to = after[h if phase == 0 else 1 - h][k % 2]
            at = ((rnd * 2 + h) * 2 + phase) * 4 + k
            mine = self.table.at[core, h]
            half = pl.ds(0, 32) if k == 2 else pl.ds(32, 32)
            if phase == 0:
                dst = mine.at[w, u, qs]
                if k < 2:
                    src = self.stage.at[qs, h]
                else:
                    src = dst = mine.at[w, down(u) if k == 2 else up(u), qs, half]
            elif k < 2:
                src = dst = mine.at[w, :, qs]
            else:
                src = dst = mine.at[down(w) if k == 2 else up(w), :, qs, half]
            return remote(src, dst, self.ssem.at[at], self.rsem.at[at], to)

        def keep(self, rnd, h):
            first, last = self.rounds[rnd]
            qs = pl.ds(first, last - first)
            u, w = (y, z) if h == 0 else (z, y)
            return pltpu.make_async_copy(
                self.stage.at[qs, h], self.table.at[core, h, w, u, qs], self.lsem.at[rnd * 2 + h]
            )

        def over(self, rnd, h):
            first, last = self.rounds[rnd]
            half = self.table.at[core, h, :, :, pl.ds(first, last - first)]
            at = len(self.rounds) * 16 + rnd * 2 + h
            return remote(half, half, self.ssem.at[at], self.rsem.at[at], beside)

        def start(self, rnd, phase):
            for k in range(2):
                for h in range(2):
                    self.hop(rnd, h, phase, k).start()

        def forward(self, rnd, phase):
            for k in range(2):
                for h in range(2):
                    self.hop(rnd, h, phase, k).wait_recv()
                    self.hop(rnd, h, phase, k + 2).start()

        def arrived(self, rnd, phase):
            for h in range(2):
                for k in (2, 3):
                    self.hop(rnd, h, phase, k).wait_recv()

        def begin(self, rnd):
            for h in range(2):
                self.keep(rnd, h).start()
            self.start(rnd, 0)

        def second(self, rnd):
            self.arrived(rnd, 0)
            for h in range(2):
                self.keep(rnd, h).wait()
            self.start(rnd, 1)

        def finish(self, rnd):
            self.arrived(rnd, 1)
            for h in range(2):
                self.over(rnd, h).start()

        def have(self):
            for rnd in range(len(self.rounds)):
                for h in range(2):
                    self.over(rnd, h).wait_recv()

        def drain(self):
            for rnd in range(len(self.rounds)):
                for h in range(2):
                    self.over(rnd, h).wait_send()
                    for phase in range(2):
                        for k in range(4):
                            self.hop(rnd, h, phase, k).wait_send()

    first_table = Gather(tab1, stage1, ROUNDS, l1, s1, r1)
    second_table = Gather(tab2, stage2, ((0, 4),), l2, s2, r2)
    first_column = pl.multiple_of(sub * 256, 256)

    def project(q, at):
        value = jnp.dot(at[...], rot[...], preferred_element_type=F32)
        stage1[q] = value.astype(BF16).reshape(2, 64, 2, 128)

    def columns(q, at):
        stage2[q] = at[:, pl.ds(first_column, 256)].reshape(2, 64, 2, 128)

    def share_codes(p):
        return remote(
            codes, every_codes.at[sub], cs.at[p], cr.at[sub], (row, lax.rem(sub + p, SUBS))
        )

    def shared_codes(p):
        source = lax.rem(sub + p, SUBS)
        return remote(codes, every_codes.at[source], cs.at[p], cr.at[source], (row, source))

    exchange(0).start()
    exchange(1).start()
    project(0, c)
    first_table.begin(0)
    own_codes = pltpu.make_async_copy(codes, every_codes.at[sub], cr.at[sub])
    own_codes.start()
    columns(0, c)
    turn_rows(2, 4)
    for k in range(2):
        exchange(k).wait_recv()
        exchange(k + 2).start()
    first_table.forward(0, 0)
    project(1, near.at[0])
    project(2, near.at[1])
    first_table.begin(1)
    first_table.second(0)
    exchange(2).wait_recv()
    exchange(3).wait_recv()
    project(3, near.at[2])
    first_table.begin(2)
    first_table.forward(1, 0)
    first_table.second(1)
    first_table.forward(2, 0)
    first_table.second(2)
    for p in range(1, SUBS):
        share_codes(p).start()
    first_table.forward(0, 1)
    turn_rows(4, 6)
    for q in range(3):
        columns(q + 1, near.at[q])
    first_table.finish(0)
    first_table.forward(1, 1)
    turn_rows(6, 8)
    first_table.finish(1)
    first_table.forward(2, 1)
    second_table.begin(0)
    acc[...] = jnp.zeros_like(acc)
    first_table.finish(2)
    first_table.have()
    second_table.forward(0, 0)

    def gather_rows(table, base, count, at):
        flat = table.reshape(16384, 2, 128)
        for s in range(0, count, 32):
            rows = [flat[ids[base + s + j]] for j in range(32)]
            for j in range(32):
                got[at + s + j] = rows[j]

    def gather_tile(table, i):
        def body(s, carry):
            gather_rows(table, i * TILE + s * 32, 32, s * 32)
            return carry

        lax.fori_loop(0, TILE // 32, body, 0)

    high = lax.broadcasted_iota(I32, (64, TILE), 0)
    low = lax.broadcasted_iota(I32, (4, TILE), 0)
    gather_tile(tab1, 0)

    def sum_tile(i, carry):
        @pl.when(i == 1)
        def _():
            second_table.second(0)

        @pl.when(i == 5)
        def _():
            second_table.forward(0, 1)

        at = pl.multiple_of(i * TILE, TILE)
        fetched = got[...].reshape(TILE, 256).astype(F32)
        rotated = vr[pl.ds(at, TILE), :] - fetched
        for h in range(2):
            turned[h * 128:(h + 1) * 128, :] = rotated[:, h * 128:(h + 1) * 128].T.astype(BF16)
        ahead = jnp.minimum(i + 1, TILES - 1) * TILE
        for grp in range(4):
            a, b, n = [], [], []
            for m in range(4 * grp, 4 * grp + 4):
                code = codes[m // 8, m % 8:m % 8 + 1, pl.ds(at, TILE)]
                a.append((high == (code & 63)).astype(BF16))
                mine = (low == (code >> 6)).astype(BF16)
                for l in range(4):
                    b.append(turned[m * 16:(m + 1) * 16, :] * mine[l:l + 1, :])
                n.append(mine)
            acc[grp] += nt(jnp.concatenate(b + n, axis=0), jnp.concatenate(a, axis=0))
            gather_rows(tab1, ahead + grp * 256, 256, grp * 256)
        return carry

    lax.fori_loop(0, TILES, sum_tile, 0)
    lane = lax.broadcasted_iota(I32, (1, 128), 1)
    for grp in range(4):
        for pair in range(2):
            cols = slice(pair * 128, pair * 128 + 128)
            m = 2 * pair
            both = jnp.where(
                lane < 64, acc[grp, m * 64:(m + 1) * 64, cols],
                acc[grp, (m + 1) * 64:(m + 2) * 64, cols],
            )
            count = jnp.where(
                lane < 64, acc[grp, 256 + m * 4:256 + m * 4 + 4, cols],
                acc[grp, 256 + m * 4 + 4:256 + m * 4 + 8, cols],
            )
            for l in range(4):
                at = (2 * grp + pair) * 4 + l
                part[at, :16, :] = both[l * 16:(l + 1) * 16, :]
                part[at, 16:, :] = jnp.broadcast_to(count[l:l + 1, :], (8, 128))

    def each(f, first=1):
        def body(p, carry):
            f(p)
            return carry

        lax.fori_loop(first, ROWS, body, 0)

    def scatter(p):
        to = lax.rem(row + p, ROWS)
        return remote(part.at[to], partgot.at[row], ps.at[p], pr.at[row], (to, sub))

    def scattered(p):
        source = lax.rem(row + p, ROWS)
        return remote(part.at[source], partgot.at[source], ps.at[p], pr.at[source], (source, sub))

    def give(p):
        to = lax.rem(row + p, ROWS)
        return remote(bchunk, rounded.at[row], bs.at[p], br.at[row], (to, sub))

    def given(p):
        source = lax.rem(row + p, ROWS)
        return remote(bchunk, rounded.at[source], bs.at[p], br.at[source], (source, sub))

    def publish(p):
        to = lax.rem(row + p, ROWS)
        return remote(chunk, means.at[row], ms.at[p], mr.at[row], (to, sub))

    def published(p):
        source = lax.rem(row + p, ROWS)
        return remote(chunk, means.at[source], ms.at[p], mr.at[source], (source, sub))

    def spread_books(p):
        to = (row, lax.rem(sub + p, SUBS))
        return remote(rounded, every.at[sub], ys.at[p], yr.at[sub], to)

    def spread_got(p):
        source = lax.rem(sub + p, SUBS)
        return remote(rounded, every.at[source], ys.at[p], yr.at[source], (row, source))

    def column_copy(i):
        return pltpu.make_async_copy(
            v.at[pl.ds(i * TILE, TILE), pl.ds(first_column, 256)],
            vcol.at[lax.rem(i, 2)], vcsem.at[lax.rem(i, 2)],
        )

    def residuals(first, last):
        def body(i, carry):
            gather_tile(tab2, i)
            column_copy(i).wait()

            @pl.when(i + 1 < TILES)
            def _():
                column_copy(i + 1).start()

            fetched = got[...].reshape(TILE, 256).astype(F32)
            value = (vcol[lax.rem(i, 2)].astype(F32) - fetched).T
            resid[:, pl.ds(pl.multiple_of(i * TILE, TILE), TILE)] = value.astype(BF16)
            return carry

        lax.fori_loop(first, last, body, 0)

    each(lambda p: scatter(p).start())
    column_copy(0).start()
    second_table.finish(0)

    def add(p, value):
        scattered(p).wait_recv()
        return value + partgot[lax.rem(row + p, ROWS)]

    value = lax.fori_loop(1, ROWS, add, part[row])
    mean = value[:16, :] / value[16:17, :]
    chunk[...] = mean
    bchunk[...] = mean.astype(BF16)
    means[row] = mean
    rounded[row] = mean.astype(BF16)
    each(lambda p: give(p).start())
    second_table.have()
    residuals(0, 4)
    each(lambda p: given(p).wait_recv())
    every[sub] = rounded[...]
    for p in range(1, SUBS):
        spread_books(p).start()
    each(lambda p: publish(p).start())
    residuals(4, 8)
    own_codes.wait()

    def send_piece(p, r):
        s = lax.rem(sub + p, SUBS)
        return remote(
            piece.at[r, p], piecegot.at[row], ws.at[p * 8 + r], wr.at[row], (sub * 8 + r, s)
        )

    def to_me(p, r):
        return jnp.logical_and(sub * 8 + r == row, p == 0)

    for p in range(SUBS):
        s = lax.rem(sub + p, SUBS)
        if p:
            spread_got(p).wait_recv()
            shared_codes(p).wait_recv()

        def relay(q, carry):
            for half in range(2):
                left = every[s, q * 4 + 2 * half].astype(F32)
                right = every[s, q * 4 + 2 * half + 1].astype(F32)
                books[2 * q, half] = jnp.where(lane < 64, left, pltpu.roll(right, 64, 1))
                books[2 * q + 1, half] = jnp.where(lane < 64, pltpu.roll(left, 64, 1), right)
            return carry

        lax.fori_loop(0, 8, relay, 0)
        total[...] = jnp.zeros_like(total)

        def cross_tile(i, carry):
            for quarter in range(TILE // 256):
                built = []
                at = pl.multiple_of(i * TILE + quarter * 256, 256)
                for m in range(16):
                    pieces = []
                    for t in range(2):
                        cols = pl.ds(pl.multiple_of(at + t * 128, 128), 128)
                        code = jnp.broadcast_to(every_codes[s, m // 8, m % 8:m % 8 + 1, cols], (8, 128))
                        inner = code & 127
                        both = []
                        for d in range(2):
                            low_half = books[m, 0, d * 8:(d + 1) * 8, :]
                            high_half = books[m, 1, d * 8:(d + 1) * 8, :]
                            both.append(jnp.where(
                                code >= 128,
                                jnp.take_along_axis(high_half, inner, axis=1),
                                jnp.take_along_axis(low_half, inner, axis=1),
                            ))
                        pieces.append(jnp.concatenate(both, axis=0).astype(BF16))
                    built.append(jnp.concatenate(pieces, axis=1))
                total[...] += nt(resid[:, pl.ds(at, 256)], jnp.concatenate(built, axis=0))
            return carry

        lax.fori_loop(0, TILES, cross_tile, 0)
        for r in range(8):
            piece[r, p] = (total[r * 32:(r + 1) * 32, :] * (1.0 / KS)).astype(BF16)
        for r in range(8):
            if p:
                send_piece(p, r).start()
            else:
                @pl.when(to_me(p, r))
                def _():
                    pltpu.make_async_copy(piece.at[r, p], piecegot.at[row], wr.at[row]).start()

                @pl.when(jnp.logical_not(to_me(p, r)))
                def _():
                    send_piece(p, r).start()

    def collect(p, value):
        source = lax.rem(row + p, ROWS)
        pltpu.make_async_copy(piece.at[0, 0], piecegot.at[source], wr.at[source]).wait()
        return value + piecegot[source].astype(F32)

    cross[...] = lax.fori_loop(0, ROWS, collect, jnp.zeros(cross.shape, F32))

    for k in range(4):
        exchange(k).wait_send()
    first_table.drain()
    second_table.drain()
    for p in range(1, SUBS):
        share_codes(p).wait_send()
        spread_books(p).wait_send()
    each(lambda p: published(p).wait_recv())
    each(lambda p: scatter(p).wait_send())
    each(lambda p: give(p).wait_send())
    each(lambda p: publish(p).wait_send())
    for p in range(SUBS):
        for r in range(8):
            if p:
                send_piece(p, r).wait_send()
            else:
                @pl.when(jnp.logical_not(to_me(p, r)))
                def _():
                    send_piece(p, r).wait_send()


def step_call(ids, vectors, centroids, rotation, codes):
    vmem = pl.BlockSpec(memory_space=pltpu.VMEM)
    dma = pltpu.SemaphoreType.DMA
    return pl.pallas_call(
        step_kernel,
        out_shape=(
            jax.ShapeDtypeStruct((ROWS, 16, 128), F32),
            jax.ShapeDtypeStruct((32, 256), F32),
        ),
        in_specs=[
            pl.BlockSpec(memory_space=pltpu.SMEM),
            pl.BlockSpec(memory_space=pl.ANY),
            vmem, vmem, vmem,
        ],
        out_specs=(vmem, vmem),
        scratch_shapes=[
            pltpu.VMEM(TABLE, BF16),
            pltpu.VMEM(TABLE, BF16),
            pltpu.VMEM((3, 128, 1024), BF16),
            pltpu.VMEM((4, 2, 64, 2, 128), BF16),
            pltpu.VMEM((4, 2, 64, 2, 128), BF16),
            pltpu.VMEM((2, TILE, 1024), BF16),
            pltpu.VMEM((TILE * TILES, 256), F32),
            pltpu.VMEM((TILE, 2, 128), BF16),
            pltpu.VMEM((256, TILE), BF16),
            pltpu.VMEM((4, 272, 256), F32),
            pltpu.VMEM((ROWS, 24, 128), F32),
            pltpu.VMEM((ROWS, 24, 128), F32),
            pltpu.VMEM((16, 128), F32),
            pltpu.VMEM((16, 128), BF16),
            pltpu.VMEM((ROWS, 16, 128), BF16),
            pltpu.VMEM((SUBS, ROWS, 16, 128), BF16),
            pltpu.VMEM((16, 2, 16, 128), F32),
            pltpu.VMEM((SUBS, 2, 8, TILE * TILES), I32),
            pltpu.VMEM((256, TILE * TILES), BF16),
            pltpu.VMEM((2, TILE, 256), BF16),
            pltpu.VMEM((256, 256), F32),
            pltpu.VMEM((8, SUBS, 32, 256), BF16),
            pltpu.VMEM((ROWS, 32, 256), BF16),
            dma((2,)), dma((4,)), dma((4,)),
            dma((6,)), dma((54,)), dma((54,)),
            dma((2,)), dma((18,)), dma((18,)),
            dma((SUBS,)), dma((SUBS,)),
            dma((ROWS,)), dma((ROWS,)),
            dma((ROWS,)), dma((ROWS,)),
            dma((ROWS,)), dma((ROWS,)),
            dma((SUBS,)), dma((SUBS,)),
            dma((ROWS,)), dma((ROWS,)),
            dma((2,)),
        ],
        compiler_params=pltpu.CompilerParams(
            collective_id=1, has_side_effects=True, vmem_limit_bytes=56 * MIB
        ),
        cost_estimate=pl.CostEstimate(
            flops=20 * 10**9, bytes_accessed=40 * 10**6, transcendentals=0
        ),
        name="step",
    )(ids, vectors, centroids, rotation, codes)


def local(vectors, list_ids, centroids, rotation, codes):
    sub = lax.axis_index("sub")
    owner, inner = list_ids // 128, list_ids % 128
    at_row, at_sub = owner // 4, owner % 4
    apart = (at_sub - sub + 4) % 4
    near = jnp.where(apart < 2, apart, 5 - apart)
    at_y, at_z, at_core = at_row // 8, (at_row // 2) % 4, at_row % 2
    half = inner // 64
    block = jnp.where(half == 0, at_z * 4 + at_y, at_y * 4 + at_z)
    ids = (((at_core * 2 + half) * 16 + block) * 4 + near) * 64 + inner % 64
    means, cross_cov = step_call(
        ids, vectors, centroids, rotation, codes.reshape(2, 8, -1)
    )
    codebooks = means.reshape(8, 4, 16, 2, 64).transpose(0, 3, 1, 4, 2).reshape(16, 256, 16)
    return codebooks, cross_cov


def solution(mesh):
    placed = (
        P("rows", None),
        P("rows"),
        P(("rows", "sub"), None),
        P(None, "sub"),
        P("sub", "rows"),
    )
    return jax.shard_map(
        local,
        mesh=mesh,
        in_specs=placed,
        out_specs=(P("sub", None, None), P("rows", "sub")),
        check_vma=False,
    )
```

```python
import jax
import jax.numpy as jnp
from jax import lax
from jax.experimental import pallas as pl
from jax.experimental.pallas import tpu as pltpu
from jax.sharding import PartitionSpec as P

KS = 256
MIB = 2**20
MESH = pl.DeviceIdType.MESH
ROWS, SUBS = 32, 4
TILE, TILES = 1024, 8
ROUNDS = ((0, 1), (1, 3), (3, 4))
F32, BF16, I32 = jnp.float32, jnp.bfloat16, jnp.int32
TABLE = (2, 2, 4, 4, 4, 64, 2, 128)


def nt(a, b):
    return lax.dot_general(a, b, (((1,), (1,)), ((), ())), preferred_element_type=F32)


def step_kernel(
    ids, v, c, rot, codes, means, cross,
    tab1, tab2, near, stage1, stage2, vbuf, vr, got, turned, acc, part, partgot,
    chunk, bchunk, rounded, every, books, every_codes, resid, vcol, total, piece, piecegot,
    vsem, xs, xr, l1, s1, r1, l2, s2, r2, cs, cr, ps, pr, ms, mr, bs, br, ys, yr, ws, wr, vcsem,
):
    row = lax.axis_index("rows")
    sub = lax.axis_index("sub")
    core = lax.rem(row, 2)
    z = lax.rem(row // 2, 4)
    y = row // 8
    block = row // 8
    own = (sub == block).astype(I32)

    def up(i):
        return lax.rem(i + 1, 4)

    def down(i):
        return lax.rem(i + 3, 4)

    def device(at_y, at_z):
        return ((at_y * 4 + at_z) * 2 + core, sub)

    beside = (row + 1 - 2 * core, sub)
    after = ((device(up(y), z), device(down(y), z)), (device(y, up(z)), device(y, down(z))))
    across = ((row, up(sub)), (row, down(sub)))

    barrier = pltpu.get_barrier_semaphore()

    def greet(p, carry):
        to = lax.rem(row + p, ROWS)

        @pl.when(p > 0)
        def _():
            pl.semaphore_signal(barrier, inc=1, device_id=(to, sub), device_id_type=MESH)

        @pl.when(jnp.logical_or(p > 0, sub != block))
        def _():
            pl.semaphore_signal(barrier, inc=1, device_id=(to, block), device_id_type=MESH)

        return carry

    lax.fori_loop(0, ROWS, greet, 0)
    for p in range(1, SUBS):
        to = (row, lax.rem(sub + p, SUBS))
        pl.semaphore_signal(barrier, inc=1, device_id=to, device_id_type=MESH)

    def remote(src, dst, send, recv, to):
        return pltpu.make_async_remote_copy(
            src_ref=src, dst_ref=dst, send_sem=send, recv_sem=recv,
            device_id=to, device_id_type=MESH,
        )

    def v_copy(i):
        return pltpu.make_async_copy(
            v.at[pl.ds(i * TILE, TILE)], vbuf.at[lax.rem(i, 2)], vsem.at[lax.rem(i, 2)]
        )

    def turn_rows(first, last):
        def body(i, carry):
            v_copy(i).wait()

            @pl.when(i + 1 < TILES)
            def _():
                v_copy(i + 1).start()

            for h in range(2):
                value = jnp.dot(
                    vbuf[lax.rem(i, 2), h * 512:(h + 1) * 512, :], rot[...],
                    preferred_element_type=F32,
                )
                vr[pl.ds(pl.multiple_of(i * TILE + h * 512, 512), 512), :] = value
            return carry

        lax.fori_loop(first, last, body, 0)

    v_copy(0).start()
    turn_rows(0, 3)
    pl.semaphore_wait(barrier, 2 * ROWS + SUBS - 2 - own)

    def exchange(k):
        half = pl.ds((0, 64, 64, 0, 0, 64)[k], 64)
        from_up = k % 2
        if k < 4:
            src, dst = c.at[half], near.at[1 - from_up, half]
        else:
            src, dst = near.at[1 - from_up, half], near.at[2, half]
        return remote(src, dst, xs.at[k], xr.at[k], across[from_up])

    class Gather:
        def __init__(self, table, stage, rounds, lsem, ssem, rsem):
            self.table, self.stage, self.rounds = table, stage, rounds
            self.lsem, self.ssem, self.rsem = lsem, ssem, rsem

        def hop(self, rnd, h, phase, k):
            first, last = self.rounds[rnd]
            qs = pl.ds(first, last - first)
            u, w = (y, z) if h == 0 else (z, y)
            to = after[h if phase == 0 else 1 - h][k % 2]
            at = ((rnd * 2 + h) * 2 + phase) * 4 + k
            mine = self.table.at[core, h]
            half = pl.ds(0, 32) if k == 2 else pl.ds(32, 32)
            if phase == 0:
                dst = mine.at[w, u, qs]
                if k < 2:
                    src = self.stage.at[qs, h]
                else:
                    src = dst = mine.at[w, down(u) if k == 2 else up(u), qs, half]
            elif k < 2:
                src = dst = mine.at[w, :, qs]
            else:
                src = dst = mine.at[down(w) if k == 2 else up(w), :, qs, half]
            return remote(src, dst, self.ssem.at[at], self.rsem.at[at], to)

        def keep(self, rnd, h):
            first, last = self.rounds[rnd]
            qs = pl.ds(first, last - first)
            u, w = (y, z) if h == 0 else (z, y)
            return pltpu.make_async_copy(
                self.stage.at[qs, h], self.table.at[core, h, w, u, qs], self.lsem.at[rnd * 2 + h]
            )

        def over(self, rnd, h, j):
            first, last = self.rounds[rnd]
            w = z if h == 0 else y
            w = (w, down(w), up(w), lax.rem(w + 2, 4))[j]
            blocks = self.table.at[core, h, w, :, pl.ds(first, last - first)]
            at = len(self.rounds) * 16 + (rnd * 2 + h) * 4 + j
            return remote(blocks, blocks, self.ssem.at[at], self.rsem.at[at], beside)

        def start(self, rnd, phase):
            for k in range(2):
                for h in range(2):
                    self.hop(rnd, h, phase, k).start()

        def forward(self, rnd, phase):
            for k in range(2):
                for h in range(2):
                    self.hop(rnd, h, phase, k).wait_recv()
                    self.hop(rnd, h, phase, k + 2).start()
                    if phase == 1:
                        self.over(rnd, h, k + 1).start()

        def arrived(self, rnd, phase):
            for h in range(2):
                for k in (2, 3):
                    self.hop(rnd, h, phase, k).wait_recv()

        def begin(self, rnd):
            for h in range(2):
                self.keep(rnd, h).start()
            self.start(rnd, 0)

        def second(self, rnd):
            self.arrived(rnd, 0)
            for h in range(2):
                self.keep(rnd, h).wait()
            self.start(rnd, 1)
            for h in range(2):
                self.over(rnd, h, 0).start()

        def finish(self, rnd):
            self.arrived(rnd, 1)
            for h in range(2):
                self.over(rnd, h, 3).start()

        def have(self):
            for rnd in range(len(self.rounds)):
                for h in range(2):
                    for j in range(4):
                        self.over(rnd, h, j).wait_recv()

        def drain(self):
            for rnd in range(len(self.rounds)):
                for h in range(2):
                    for j in range(4):
                        self.over(rnd, h, j).wait_send()
                    for phase in range(2):
                        for k in range(4):
                            self.hop(rnd, h, phase, k).wait_send()

    first_table = Gather(tab1, stage1, ROUNDS, l1, s1, r1)
    second_table = Gather(tab2, stage2, ((0, 1), (1, 4)), l2, s2, r2)
    first_column = pl.multiple_of(sub * 256, 256)

    def project(q, at):
        value = jnp.dot(at[...], rot[...], preferred_element_type=F32)
        stage1[q] = value.astype(BF16).reshape(2, 64, 2, 128)

    def columns(q, at):
        stage2[q] = at[:, pl.ds(first_column, 256)].reshape(2, 64, 2, 128)

    def share_codes(p):
        return remote(
            codes, every_codes.at[sub], cs.at[p], cr.at[sub], (row, lax.rem(sub + p, SUBS))
        )

    def shared_codes(p):
        source = lax.rem(sub + p, SUBS)
        return remote(codes, every_codes.at[source], cs.at[p], cr.at[source], (row, source))

    for k in range(4):
        exchange(k).start()
    project(0, c)
    first_table.begin(0)
    columns(0, c)
    second_table.begin(0)
    own_codes = pltpu.make_async_copy(codes, every_codes.at[sub], cr.at[sub])
    own_codes.start()
    first_table.forward(0, 0)
    second_table.forward(0, 0)
    first_table.second(0)
    second_table.second(0)
    for k in range(2):
        exchange(k).wait_recv()
        exchange(k + 4).start()
    turn_rows(3, 4)
    exchange(2).wait_recv()
    exchange(3).wait_recv()
    project(1, near.at[0])
    project(2, near.at[1])
    first_table.begin(1)
    first_table.forward(0, 1)
    exchange(4).wait_recv()
    exchange(5).wait_recv()
    project(3, near.at[2])
    first_table.begin(2)
    first_table.forward(1, 0)
    first_table.second(1)
    first_table.forward(2, 0)
    first_table.second(2)
    for p in range(1, SUBS):
        share_codes(p).start()
    first_table.finish(0)
    second_table.forward(0, 1)
    for q in range(3):
        columns(q + 1, near.at[q])
    turn_rows(4, 6)
    second_table.finish(0)
    first_table.forward(1, 1)
    turn_rows(6, 8)
    first_table.finish(1)
    first_table.forward(2, 1)
    second_table.begin(1)
    acc[...] = jnp.zeros_like(acc)
    first_table.finish(2)
    first_table.have()
    second_table.forward(1, 0)

    def gather_rows(table, base, count, at):
        flat = table.reshape(16384, 2, 128)
        for s in range(0, count, 32):
            rows = [flat[ids[base + s + j]] for j in range(32)]
            for j in range(32):
                got[at + s + j] = rows[j]

    def gather_tile(table, i):
        def body(s, carry):
            gather_rows(table, i * TILE + s * 32, 32, s * 32)
            return carry

        lax.fori_loop(0, TILE // 32, body, 0)

    high = lax.broadcasted_iota(I32, (64, TILE), 0)
    low = lax.broadcasted_iota(I32, (4, TILE), 0)
    gather_tile(tab1, 0)

    def sum_tile(i, carry):
        @pl.when(i == 1)
        def _():
            second_table.second(1)

        @pl.when(i == 6)
        def _():
            second_table.forward(1, 1)

        at = pl.multiple_of(i * TILE, TILE)
        fetched = got[...].reshape(TILE, 256).astype(F32)
        rotated = vr[pl.ds(at, TILE), :] - fetched
        for h in range(2):
            turned[h * 128:(h + 1) * 128, :] = rotated[:, h * 128:(h + 1) * 128].T.astype(BF16)
        ahead = jnp.minimum(i + 1, TILES - 1) * TILE
        for grp in range(4):
            a, b, n = [], [], []
            for m in range(4 * grp, 4 * grp + 4):
                code = codes[m // 8, m % 8:m % 8 + 1, pl.ds(at, TILE)]
                a.append((high == (code & 63)).astype(BF16))
                mine = (low == (code >> 6)).astype(BF16)
                for l in range(4):
                    b.append(turned[m * 16:(m + 1) * 16, :] * mine[l:l + 1, :])
                n.append(mine)
            acc[grp] += nt(jnp.concatenate(b + n, axis=0), jnp.concatenate(a, axis=0))
            gather_rows(tab1, ahead + grp * 256, 256, grp * 256)
        return carry

    lax.fori_loop(0, TILES, sum_tile, 0)
    lane = lax.broadcasted_iota(I32, (1, 128), 1)
    for grp in range(4):
        for pair in range(2):
            cols = slice(pair * 128, pair * 128 + 128)
            m = 2 * pair
            both = jnp.where(
                lane < 64, acc[grp, m * 64:(m + 1) * 64, cols],
                acc[grp, (m + 1) * 64:(m + 2) * 64, cols],
            )
            count = jnp.where(
                lane < 64, acc[grp, 256 + m * 4:256 + m * 4 + 4, cols],
                acc[grp, 256 + m * 4 + 4:256 + m * 4 + 8, cols],
            )
            for l in range(4):
                at = (2 * grp + pair) * 4 + l
                part[at, :16, :] = both[l * 16:(l + 1) * 16, :]
                part[at, 16:17, :] = count[l:l + 1, :]

    def each(f, first=1):
        def body(p, carry):
            f(p)
            return carry

        lax.fori_loop(first, ROWS, body, 0)

    def scatter(p):
        to = lax.rem(row + p, ROWS)
        return remote(
            part.at[to, pl.ds(0, 17)], partgot.at[row, pl.ds(0, 17)], ps.at[p], pr.at[row], (to, sub)
        )

    def scattered(p):
        source = lax.rem(row + p, ROWS)
        return remote(
            part.at[source, pl.ds(0, 17)], partgot.at[source, pl.ds(0, 17)], ps.at[p], pr.at[source],
            (source, sub),
        )

    def give(p):
        to = lax.rem(row + p, ROWS)
        return remote(bchunk, rounded.at[row], bs.at[p], br.at[row], (to, sub))

    def given(p):
        source = lax.rem(row + p, ROWS)
        return remote(bchunk, rounded.at[source], bs.at[p], br.at[source], (source, sub))

    def publish(p):
        to = lax.rem(row + p, ROWS)
        return remote(chunk, means.at[row], ms.at[p], mr.at[row], (to, sub))

    def published(p):
        source = lax.rem(row + p, ROWS)
        return remote(chunk, means.at[source], ms.at[p], mr.at[source], (source, sub))

    def spread_books(p):
        to = (row, lax.rem(sub + p, SUBS))
        return remote(rounded, every.at[sub], ys.at[p], yr.at[sub], to)

    def spread_got(p):
        source = lax.rem(sub + p, SUBS)
        return remote(rounded, every.at[source], ys.at[p], yr.at[source], (row, source))

    def column_copy(i):
        return pltpu.make_async_copy(
            v.at[pl.ds(i * TILE, TILE), pl.ds(first_column, 256)],
            vcol.at[lax.rem(i, 2)], vcsem.at[lax.rem(i, 2)],
        )

    each(lambda p: scatter(p).start())
    column_copy(0).start()
    second_table.finish(1)

    def add(p, value):
        scattered(p).wait_recv()
        return value + partgot[lax.rem(row + p, ROWS), :17, :]

    value = lax.fori_loop(1, ROWS, add, part[row, :17, :])
    mean = value[:16, :] / value[16:17, :]
    chunk[...] = mean
    bchunk[...] = mean.astype(BF16)
    means[row] = mean
    rounded[row] = mean.astype(BF16)
    each(lambda p: give(p).start())
    second_table.have()
    gather_tile(tab2, 0)
    each(lambda p: given(p).wait_recv())
    every[sub] = rounded[...]
    for p in range(1, SUBS):
        spread_books(p).start()
    each(lambda p: publish(p).start())
    own_codes.wait()

    def send_piece(p, r):
        s = lax.rem(sub + p, SUBS)
        return remote(
            piece.at[r, p], piecegot.at[row], ws.at[p * 8 + r], wr.at[row], (sub * 8 + r, s)
        )

    def to_me(p, r):
        return jnp.logical_and(sub * 8 + r == row, p == 0)

    for p in range(SUBS):
        s = lax.rem(sub + p, SUBS)
        if p:
            spread_got(p).wait_recv()
            shared_codes(p).wait_recv()

        def relay(q, carry):
            for half in range(2):
                left = every[s, q * 4 + 2 * half].astype(F32)
                right = every[s, q * 4 + 2 * half + 1].astype(F32)
                books[2 * q, half] = jnp.where(lane < 64, left, pltpu.roll(right, 64, 1))
                books[2 * q + 1, half] = jnp.where(lane < 64, pltpu.roll(left, 64, 1), right)
            return carry

        lax.fori_loop(0, 8, relay, 0)
        total[...] = jnp.zeros_like(total)

        def cross_tile(i, carry):
            if p == 0:
                column_copy(i).wait()

                @pl.when(i + 1 < TILES)
                def _():
                    column_copy(i + 1).start()

                fetched = got[...].reshape(TILE, 256).astype(F32)
                value = (vcol[lax.rem(i, 2)].astype(F32) - fetched).T
                resid[:, pl.ds(pl.multiple_of(i * TILE, TILE), TILE)] = value.astype(BF16)
                ahead = jnp.minimum(i + 1, TILES - 1) * TILE

            for quarter in range(TILE // 256):
                built = []
                at = pl.multiple_of(i * TILE + quarter * 256, 256)
                for m in range(16):
                    pieces = []
                    for t in range(2):
                        cols = pl.ds(pl.multiple_of(at + t * 128, 128), 128)
                        code = jnp.broadcast_to(every_codes[s, m // 8, m % 8:m % 8 + 1, cols], (8, 128))
                        inner = code & 127
                        both = []
                        for d in range(2):
                            low_half = books[m, 0, d * 8:(d + 1) * 8, :]
                            high_half = books[m, 1, d * 8:(d + 1) * 8, :]
                            both.append(jnp.where(
                                code >= 128,
                                jnp.take_along_axis(high_half, inner, axis=1),
                                jnp.take_along_axis(low_half, inner, axis=1),
                            ))
                        pieces.append(jnp.concatenate(both, axis=0).astype(BF16))
                    built.append(jnp.concatenate(pieces, axis=1))
                total[...] += nt(resid[:, pl.ds(at, 256)], jnp.concatenate(built, axis=0))
                if p == 0:
                    gather_rows(tab2, ahead + quarter * 256, 256, quarter * 256)
            return carry

        lax.fori_loop(0, TILES, cross_tile, 0)
        for r in range(8):
            piece[r, p] = (total[r * 32:(r + 1) * 32, :] * (1.0 / KS)).astype(BF16)
        for r in range(8):
            if p:
                send_piece(p, r).start()
            else:
                @pl.when(to_me(p, r))
                def _():
                    pltpu.make_async_copy(piece.at[r, p], piecegot.at[row], wr.at[row]).start()

                @pl.when(jnp.logical_not(to_me(p, r)))
                def _():
                    send_piece(p, r).start()

    def collect(p, value):
        source = lax.rem(row + p, ROWS)
        pltpu.make_async_copy(piece.at[0, 0], piecegot.at[source], wr.at[source]).wait()
        return value + piecegot[source].astype(F32)

    cross[...] = lax.fori_loop(0, ROWS, collect, jnp.zeros(cross.shape, F32))

    for k in range(6):
        exchange(k).wait_send()
    first_table.drain()
    second_table.drain()
    for p in range(1, SUBS):
        share_codes(p).wait_send()
        spread_books(p).wait_send()
    each(lambda p: published(p).wait_recv())
    each(lambda p: scatter(p).wait_send())
    each(lambda p: give(p).wait_send())
    each(lambda p: publish(p).wait_send())
    for p in range(SUBS):
        for r in range(8):
            if p:
                send_piece(p, r).wait_send()
            else:
                @pl.when(jnp.logical_not(to_me(p, r)))
                def _():
                    send_piece(p, r).wait_send()


def step_call(ids, vectors, centroids, rotation, codes):
    vmem = pl.BlockSpec(memory_space=pltpu.VMEM)
    dma = pltpu.SemaphoreType.DMA
    return pl.pallas_call(
        step_kernel,
        out_shape=(
            jax.ShapeDtypeStruct((ROWS, 16, 128), F32),
            jax.ShapeDtypeStruct((32, 256), F32),
        ),
        in_specs=[
            pl.BlockSpec(memory_space=pltpu.SMEM),
            pl.BlockSpec(memory_space=pl.ANY),
            vmem, vmem, vmem,
        ],
        out_specs=(vmem, vmem),
        scratch_shapes=[
            pltpu.VMEM(TABLE, BF16),
            pltpu.VMEM(TABLE, BF16),
            pltpu.VMEM((3, 128, 1024), BF16),
            pltpu.VMEM((4, 2, 64, 2, 128), BF16),
            pltpu.VMEM((4, 2, 64, 2, 128), BF16),
            pltpu.VMEM((2, TILE, 1024), BF16),
            pltpu.VMEM((TILE * TILES, 256), F32),
            pltpu.VMEM((TILE, 2, 128), BF16),
            pltpu.VMEM((256, TILE), BF16),
            pltpu.VMEM((4, 272, 256), F32),
            pltpu.VMEM((ROWS, 24, 128), F32),
            pltpu.VMEM((ROWS, 24, 128), F32),
            pltpu.VMEM((16, 128), F32),
            pltpu.VMEM((16, 128), BF16),
            pltpu.VMEM((ROWS, 16, 128), BF16),
            pltpu.VMEM((SUBS, ROWS, 16, 128), BF16),
            pltpu.VMEM((16, 2, 16, 128), F32),
            pltpu.VMEM((SUBS, 2, 8, TILE * TILES), I32),
            pltpu.VMEM((256, TILE * TILES), BF16),
            pltpu.VMEM((2, TILE, 256), BF16),
            pltpu.VMEM((256, 256), F32),
            pltpu.VMEM((8, SUBS, 32, 256), BF16),
            pltpu.VMEM((ROWS, 32, 256), BF16),
            dma((2,)), dma((6,)), dma((6,)),
            dma((6,)), dma((72,)), dma((72,)),
            dma((4,)), dma((48,)), dma((48,)),
            dma((SUBS,)), dma((SUBS,)),
            dma((ROWS,)), dma((ROWS,)),
            dma((ROWS,)), dma((ROWS,)),
            dma((ROWS,)), dma((ROWS,)),
            dma((SUBS,)), dma((SUBS,)),
            dma((ROWS,)), dma((ROWS,)),
            dma((2,)),
        ],
        compiler_params=pltpu.CompilerParams(
            collective_id=1, has_side_effects=True, vmem_limit_bytes=56 * MIB
        ),
        cost_estimate=pl.CostEstimate(
            flops=20 * 10**9, bytes_accessed=40 * 10**6, transcendentals=0
        ),
        name="step",
    )(ids, vectors, centroids, rotation, codes)


def local(vectors, list_ids, centroids, rotation, codes):
    sub = lax.axis_index("sub")
    owner, inner = list_ids // 128, list_ids % 128
    at_row, at_sub = owner // 4, owner % 4
    apart = (at_sub - sub + 4) % 4
    near = jnp.where(apart < 2, apart, 5 - apart)
    at_y, at_z, at_core = at_row // 8, (at_row // 2) % 4, at_row % 2
    half = inner // 64
    block = jnp.where(half == 0, at_z * 4 + at_y, at_y * 4 + at_z)
    ids = (((at_core * 2 + half) * 16 + block) * 4 + near) * 64 + inner % 64
    means, cross_cov = step_call(
        ids, vectors, centroids, rotation, codes.reshape(2, 8, -1)
    )
    codebooks = means.reshape(8, 4, 16, 2, 64).transpose(0, 3, 1, 4, 2).reshape(16, 256, 16)
    return codebooks, cross_cov


def solution(mesh):
    placed = (
        P("rows", None),
        P("rows"),
        P(("rows", "sub"), None),
        P(None, "sub"),
        P("sub", "rows"),
    )
    return jax.shard_map(
        local,
        mesh=mesh,
        in_specs=placed,
        out_specs=(P("sub", None, None), P("rows", "sub")),
        check_vma=False,
    )
```

```python
import jax
import jax.numpy as jnp
from jax import lax
from jax.experimental import pallas as pl
from jax.experimental.pallas import tpu as pltpu
from jax.sharding import PartitionSpec as P

KS = 256
MIB = 2**20
MESH = pl.DeviceIdType.MESH
ROWS, SUBS = 32, 4
TILE, TILES = 1024, 8
ROUNDS = ((0, 1), (1, 3), (3, 4))
F32, BF16, I32 = jnp.float32, jnp.bfloat16, jnp.int32
TABLE = (2, 2, 4, 4, 4, 64, 2, 128)


def nt(a, b):
    return lax.dot_general(a, b, (((1,), (1,)), ((), ())), preferred_element_type=F32)


def step_kernel(
    ids, v, c, rot, codes, outbooks, cross,
    tab1, tab2, near, stage1, stage2, vbuf, vr, got, turned, acc, part, partgot, means,
    chunk, bchunk, rounded, every, books, every_codes, resid, vcol, total, piece, piecegot,
    vsem, xs, xr, l1, s1, r1, o1, l2, s2, r2, o2, cs, cr, ps, pr, ms, mr, bs, br, ys, yr, ws, wr,
    vcsem,
):
    row = lax.axis_index("rows")
    sub = lax.axis_index("sub")
    core = lax.rem(row, 2)
    z = lax.rem(row // 2, 4)
    y = row // 8
    block = row // 8

    def up(i):
        return lax.rem(i + 1, 4)

    def down(i):
        return lax.rem(i + 3, 4)

    def device(at_y, at_z):
        return ((at_y * 4 + at_z) * 2 + core, sub)

    beside = (row + 1 - 2 * core, sub)
    after = ((device(up(y), z), device(down(y), z)), (device(y, up(z)), device(y, down(z))))
    across = ((row, up(sub)), (row, down(sub)))

    barrier = pltpu.get_barrier_semaphore()
    for peer in after[0] + after[1] + across + (beside,):
        pl.semaphore_signal(barrier, inc=1, device_id=peer, device_id_type=MESH)

    def remote(src, dst, send, recv, to):
        return pltpu.make_async_remote_copy(
            src_ref=src, dst_ref=dst, send_sem=send, recv_sem=recv,
            device_id=to, device_id_type=MESH,
        )

    def v_copy(i):
        return pltpu.make_async_copy(
            v.at[pl.ds(i * TILE, TILE)], vbuf.at[lax.rem(i, 2)], vsem.at[lax.rem(i, 2)]
        )

    def turn_rows(first, last):
        def body(i, carry):
            v_copy(i).wait()

            @pl.when(i + 1 < TILES)
            def _():
                v_copy(i + 1).start()

            for h in range(2):
                value = jnp.dot(
                    vbuf[lax.rem(i, 2), h * 512:(h + 1) * 512, :], rot[...],
                    preferred_element_type=F32,
                )
                vr[pl.ds(pl.multiple_of(i * TILE + h * 512, 512), 512), :] = value
            return carry

        lax.fori_loop(first, last, body, 0)

    v_copy(0).start()
    turn_rows(0, 3)
    pl.semaphore_wait(barrier, 7)

    def exchange(k):
        half = pl.ds((0, 64, 64, 0, 0, 64)[k], 64)
        from_up = k % 2
        if k < 4:
            src, dst = c.at[half], near.at[1 - from_up, half]
        else:
            src, dst = near.at[1 - from_up, half], near.at[2, half]
        return remote(src, dst, xs.at[k], xr.at[k], across[from_up])

    class Gather:
        def __init__(self, table, stage, rounds, lsem, ssem, rsem, osem):
            self.table, self.stage, self.rounds = table, stage, rounds
            self.lsem, self.ssem, self.rsem, self.osem = lsem, ssem, rsem, osem

        def place(self, rnd, h):
            first, last = self.rounds[rnd]
            u, w = (y, z) if h == 0 else (z, y)
            return pl.ds(first, last - first), u, w

        def hop(self, rnd, h, phase, k, j=0):
            qs, u, w = self.place(rnd, h)
            to = after[h if phase == 0 else 1 - h][k % 2]
            mine = self.table.at[core, h]
            half = pl.ds(0, 32) if k == 2 else pl.ds(32, 32)
            if phase == 0:
                if k < 2:
                    src, dst = self.stage.at[qs, h], mine.at[w, u, qs]
                else:
                    src = dst = mine.at[w, down(u) if k == 2 else up(u), qs, half]
            else:
                at = (u, down(u), up(u), lax.rem(u + 2, 4))[j]
                if k < 2:
                    src, dst = mine.at[w, at, qs], mine.at[w, at, qs]
                    if j == 0:
                        src = self.stage.at[qs, h]
                else:
                    src = dst = mine.at[down(w) if k == 2 else up(w), at, qs, half]
            number = (rnd * 2 + h) * 20 + (k if phase == 0 else 4 + 4 * j + k)
            return remote(src, dst, self.ssem.at[phase], self.rsem.at[number], to)

        def keep(self, rnd, h):
            qs, u, w = self.place(rnd, h)
            return pltpu.make_async_copy(
                self.stage.at[qs, h], self.table.at[core, h, w, u, qs], self.lsem.at[rnd * 2 + h]
            )

        def over(self, rnd, h, j):
            qs, u, w = self.place(rnd, h)
            w = (w, down(w), up(w), lax.rem(w + 2, 4))[j]
            blocks = self.table.at[core, h, w, :, qs]
            remote(blocks, blocks, self.osem.at[0], self.osem.at[1], beside).start()

        def begin(self, rnd):
            for h in range(2):
                self.keep(rnd, h).start()
            for h in range(2):
                for k in range(2):
                    self.hop(rnd, h, 0, k).start()
            for h in range(2):
                for k in range(2):
                    self.hop(rnd, h, 1, k).start()

        def sides(self, rnd):
            for k in range(2):
                for h in range(2):
                    self.hop(rnd, h, 0, k).wait_recv()
                    self.hop(rnd, h, 0, k + 2).start()
            for j in (1, 2):
                for h in range(2):
                    for k in range(2):
                        self.hop(rnd, h, 1, k, j).start()

        def opposite(self, rnd):
            for h in range(2):
                for k in (2, 3):
                    self.hop(rnd, h, 0, k).wait_recv()
                for k in range(2):
                    self.hop(rnd, h, 1, k, 3).start()
            for h in range(2):
                self.keep(rnd, h).wait()
                self.over(rnd, h, 0)

        def forward(self, rnd, *blocks):
            for j in blocks:
                for k in range(2):
                    for h in range(2):
                        self.hop(rnd, h, 1, k, j).wait_recv()
                        self.hop(rnd, h, 1, k + 2, j).start()
            if blocks[-1] == 3:
                for h in range(2):
                    self.over(rnd, h, 1)
                    self.over(rnd, h, 2)

        def finish(self, rnd):
            for h in range(2):
                for j in range(4):
                    for k in (2, 3):
                        self.hop(rnd, h, 1, k, j).wait_recv()
                self.over(rnd, h, 3)

        def all_of(self, blocks, sem):
            pltpu.make_async_copy(blocks, blocks, sem).wait()

        def have(self):
            self.all_of(self.table.at[0], self.osem.at[1])

        def drain(self):
            self.all_of(self.table.at[0, :, 0, pl.ds(0, 3)], self.ssem.at[0])
            self.all_of(self.table.at[0, :, pl.ds(0, 3)], self.ssem.at[1])
            self.all_of(self.table.at[0], self.osem.at[0])

    first_table = Gather(tab1, stage1, ROUNDS, l1, s1, r1, o1)
    second_table = Gather(tab2, stage2, ((0, 4),), l2, s2, r2, o2)
    first_column = pl.multiple_of(sub * 256, 256)

    def project(q, at):
        value = jnp.dot(at[...], rot[...], preferred_element_type=F32)
        stage1[q] = value.astype(BF16).reshape(2, 64, 2, 128)

    def columns(q, at):
        stage2[q] = at[:, pl.ds(first_column, 256)].reshape(2, 64, 2, 128)

    def share_codes(p):
        return remote(
            codes, every_codes.at[sub], cs.at[0], cr.at[sub], (row, lax.rem(sub + p, SUBS))
        )

    def shared_codes(p):
        source = lax.rem(sub + p, SUBS)
        return remote(codes, every_codes.at[source], cs.at[0], cr.at[source], (row, source))

    for k in range(4):
        exchange(k).start()
    project(0, c)
    first_table.begin(0)
    own_codes = pltpu.make_async_copy(codes, every_codes.at[sub], cr.at[sub])
    own_codes.start()
    columns(0, c)
    first_table.sides(0)
    first_table.opposite(0)
    for k in range(2):
        exchange(k).wait_recv()
        exchange(k + 4).start()
    turn_rows(3, 4)
    first_table.forward(0, 0)
    exchange(2).wait_recv()
    exchange(3).wait_recv()
    project(1, near.at[0])
    project(2, near.at[1])
    first_table.begin(1)
    first_table.forward(0, 1, 2)
    exchange(4).wait_recv()
    exchange(5).wait_recv()
    project(3, near.at[2])
    first_table.begin(2)
    first_table.sides(1)
    first_table.sides(2)
    first_table.forward(0, 3)
    turn_rows(4, 5)
    first_table.opposite(1)
    first_table.opposite(2)
    for p in range(1, SUBS):
        share_codes(p).start()
    turn_rows(5, 6)
    first_table.forward(1, 0)
    first_table.forward(2, 0)
    first_table.forward(1, 1, 2)
    first_table.forward(2, 1, 2)
    turn_rows(6, 8)
    first_table.forward(1, 3)
    first_table.forward(2, 3)
    for q in range(3):
        columns(q + 1, near.at[q])
    second_table.begin(0)
    acc[...] = jnp.zeros_like(acc)
    for rnd in range(3):
        first_table.finish(rnd)
    second_table.sides(0)
    first_table.have()

    def gather_rows(table, base, count, at):
        flat = table.reshape(16384, 2, 128)
        for s in range(0, count, 32):
            rows = [flat[ids[base + s + j]] for j in range(32)]
            for j in range(32):
                got[at + s + j] = rows[j]

    def gather_tile(table, i):
        def body(s, carry):
            gather_rows(table, i * TILE + s * 32, 32, s * 32)
            return carry

        lax.fori_loop(0, TILE // 32, body, 0)

    high = lax.broadcasted_iota(I32, (64, TILE), 0)
    low = lax.broadcasted_iota(I32, (4, TILE), 0)
    gather_tile(tab1, 0)

    def sum_tile(i, carry):
        @pl.when(i == 0)
        def _():
            second_table.opposite(0)

        @pl.when(i == 2)
        def _():
            second_table.forward(0, 0)

        @pl.when(i == 4)
        def _():
            second_table.forward(0, 1, 2)

        @pl.when(i == 7)
        def _():
            second_table.forward(0, 3)

        at = pl.multiple_of(i * TILE, TILE)
        fetched = got[...].reshape(TILE, 256).astype(F32)
        rotated = vr[pl.ds(at, TILE), :] - fetched
        for h in range(2):
            turned[h * 128:(h + 1) * 128, :] = rotated[:, h * 128:(h + 1) * 128].T.astype(BF16)
        ahead = jnp.minimum(i + 1, TILES - 1) * TILE
        for grp in range(4):
            a, b, n = [], [], []
            for m in range(4 * grp, 4 * grp + 4):
                code = codes[m // 8, m % 8:m % 8 + 1, pl.ds(at, TILE)]
                a.append((high == (code & 63)).astype(BF16))
                mine = (low == (code >> 6)).astype(BF16)
                for l in range(4):
                    b.append(turned[m * 16:(m + 1) * 16, :] * mine[l:l + 1, :])
                n.append(mine)
            acc[grp] += nt(jnp.concatenate(b + n, axis=0), jnp.concatenate(a, axis=0))
            gather_rows(tab1, ahead + grp * 256, 256, grp * 256)
        return carry

    lax.fori_loop(0, TILES, sum_tile, 0)
    lane = lax.broadcasted_iota(I32, (1, 128), 1)
    for grp in range(4):
        for pair in range(2):
            cols = slice(pair * 128, pair * 128 + 128)
            m = 2 * pair
            both = jnp.where(
                lane < 64, acc[grp, m * 64:(m + 1) * 64, cols],
                acc[grp, (m + 1) * 64:(m + 2) * 64, cols],
            )
            count = jnp.where(
                lane < 64, acc[grp, 256 + m * 4:256 + m * 4 + 4, cols],
                acc[grp, 256 + m * 4 + 4:256 + m * 4 + 8, cols],
            )
            for l in range(4):
                at = (2 * grp + pair) * 4 + l
                part[at, :16, :] = both[l * 16:(l + 1) * 16, :]
                part[at, 16:17, :] = count[l:l + 1, :]

    def each(f, first=1):
        def body(p, carry):
            f(p)
            return carry

        lax.fori_loop(first, ROWS, body, 0)

    def scatter(p):
        to = lax.rem(row + p, ROWS)
        remote(
            part.at[to, pl.ds(0, 17)], partgot.at[row, pl.ds(0, 17)], ps.at[0], pr.at[0], (to, sub)
        ).start()

    def give(p):
        to = lax.rem(row + p, ROWS)
        remote(bchunk, rounded.at[row], bs.at[0], br.at[0], (to, sub)).start()

    def publish(p):
        to = lax.rem(row + p, ROWS)
        remote(chunk, means.at[row], ms.at[0], mr.at[0], (to, sub)).start()

    def all_of(blocks, sem):
        pltpu.make_async_copy(blocks, blocks, sem).wait()

    others = pl.ds(0, ROWS - 1)

    def spread_books(p):
        to = (row, lax.rem(sub + p, SUBS))
        return remote(rounded, every.at[sub], ys.at[0], yr.at[sub], to)

    def spread_got(p):
        source = lax.rem(sub + p, SUBS)
        return remote(rounded, every.at[source], ys.at[0], yr.at[source], (row, source))

    def column_copy(i):
        return pltpu.make_async_copy(
            v.at[pl.ds(i * TILE, TILE), pl.ds(first_column, 256)],
            vcol.at[lax.rem(i, 2)], vcsem.at[lax.rem(i, 2)],
        )

    each(scatter)
    column_copy(0).start()
    partgot[row] = part[row]
    first_table.drain()
    second_table.finish(0)
    all_of(partgot.at[others, pl.ds(0, 17)], pr.at[0])
    value = jnp.sum(partgot[:, :17, :], axis=0)
    mean = value[:16, :] / value[16:17, :]
    chunk[...] = mean
    bchunk[...] = mean.astype(BF16)
    means[row] = mean
    rounded[row] = mean.astype(BF16)
    each(give)
    second_table.have()
    gather_tile(tab2, 0)
    each(publish)
    all_of(rounded.at[others], br.at[0])
    every[sub] = rounded[...]
    for p in range(1, SUBS):
        spread_books(p).start()
    own_codes.wait()

    def send_piece(p, r):
        s = lax.rem(sub + p, SUBS)
        return remote(
            piece.at[r, p], piecegot.at[row], ws.at[0], wr.at[0], (sub * 8 + r, s)
        )

    def to_me(p, r):
        return jnp.logical_and(sub * 8 + r == row, p == 0)

    for p in range(SUBS):
        s = lax.rem(sub + p, SUBS)
        if p:
            spread_got(p).wait_recv()
            shared_codes(p).wait_recv()

        def relay(q, carry):
            for half in range(2):
                left = every[s, q * 4 + 2 * half].astype(F32)
                right = every[s, q * 4 + 2 * half + 1].astype(F32)
                books[2 * q, half] = jnp.where(lane < 64, left, pltpu.roll(right, 64, 1))
                books[2 * q + 1, half] = jnp.where(lane < 64, pltpu.roll(left, 64, 1), right)
            return carry

        lax.fori_loop(0, 8, relay, 0)
        total[...] = jnp.zeros_like(total)

        def cross_tile(i, carry):
            if p == 0:
                column_copy(i).wait()

                @pl.when(i + 1 < TILES)
                def _():
                    column_copy(i + 1).start()

                fetched = got[...].reshape(TILE, 256).astype(F32)
                value = (vcol[lax.rem(i, 2)].astype(F32) - fetched).T
                resid[:, pl.ds(pl.multiple_of(i * TILE, TILE), TILE)] = value.astype(BF16)
                ahead = jnp.minimum(i + 1, TILES - 1) * TILE

            for quarter in range(TILE // 256):
                built = []
                at = pl.multiple_of(i * TILE + quarter * 256, 256)
                for m in range(16):
                    pieces = []
                    for t in range(2):
                        cols = pl.ds(pl.multiple_of(at + t * 128, 128), 128)
                        code = jnp.broadcast_to(every_codes[s, m // 8, m % 8:m % 8 + 1, cols], (8, 128))
                        inner = code & 127
                        both = []
                        for d in range(2):
                            low_half = books[m, 0, d * 8:(d + 1) * 8, :]
                            high_half = books[m, 1, d * 8:(d + 1) * 8, :]
                            both.append(jnp.where(
                                code >= 128,
                                jnp.take_along_axis(high_half, inner, axis=1),
                                jnp.take_along_axis(low_half, inner, axis=1),
                            ))
                        pieces.append(jnp.concatenate(both, axis=0).astype(BF16))
                    built.append(jnp.concatenate(pieces, axis=1))
                total[...] += nt(resid[:, pl.ds(at, 256)], jnp.concatenate(built, axis=0))
                if p == 0:
                    gather_rows(tab2, ahead + quarter * 256, 256, quarter * 256)
            return carry

        lax.fori_loop(0, TILES, cross_tile, 0)
        for r in range(8):
            piece[r, p] = (total[r * 32:(r + 1) * 32, :] * (1.0 / KS)).astype(BF16)
        for r in range(8):
            if p:
                send_piece(p, r).start()
            else:
                @pl.when(to_me(p, r))
                def _():
                    pltpu.make_async_copy(piece.at[r, p], piecegot.at[row], wr.at[0]).start()

                @pl.when(jnp.logical_not(to_me(p, r)))
                def _():
                    send_piece(p, r).start()

    for k in range(6):
        exchange(k).wait_send()
    second_table.drain()
    all_of(every_codes.at[pl.ds(0, SUBS - 1)], cs.at[0])
    all_of(every.at[pl.ds(0, SUBS - 1)], ys.at[0])
    all_of(partgot.at[others, pl.ds(0, 17)], ps.at[0])
    all_of(rounded.at[others], bs.at[0])
    all_of(means.at[others], ms.at[0])
    all_of(means.at[others], mr.at[0])

    def order(q, carry):
        for half in range(2):
            left, right = means[q * 4 + 2 * half], means[q * 4 + 2 * half + 1]
            cols = slice(half * 128, half * 128 + 128)
            outbooks[2 * q, :, cols] = jnp.where(lane < 64, left, pltpu.roll(right, 64, 1))
            outbooks[2 * q + 1, :, cols] = jnp.where(lane < 64, pltpu.roll(left, 64, 1), right)
        return carry

    lax.fori_loop(0, 8, order, 0)
    all_of(piecegot, wr.at[0])
    value = jnp.zeros(cross.shape, F32)
    for r in range(ROWS):
        value = value + piecegot[r].astype(F32)
    cross[...] = value

    @pl.when(sub == block)
    def _():
        all_of(piecegot.at[others], ws.at[0])

    @pl.when(sub != block)
    def _():
        all_of(piecegot, ws.at[0])


def step_call(ids, vectors, centroids, rotation, codes):
    vmem = pl.BlockSpec(memory_space=pltpu.VMEM)
    dma = pltpu.SemaphoreType.DMA
    return pl.pallas_call(
        step_kernel,
        out_shape=(
            jax.ShapeDtypeStruct((16, 16, 256), F32),
            jax.ShapeDtypeStruct((32, 256), F32),
        ),
        in_specs=[
            pl.BlockSpec(memory_space=pltpu.SMEM),
            pl.BlockSpec(memory_space=pl.ANY),
            vmem, vmem, vmem,
        ],
        out_specs=(vmem, vmem),
        scratch_shapes=[
            pltpu.VMEM(TABLE, BF16),
            pltpu.VMEM(TABLE, BF16),
            pltpu.VMEM((3, 128, 1024), BF16),
            pltpu.VMEM((4, 2, 64, 2, 128), BF16),
            pltpu.VMEM((4, 2, 64, 2, 128), BF16),
            pltpu.VMEM((2, TILE, 1024), BF16),
            pltpu.VMEM((TILE * TILES, 256), F32),
            pltpu.VMEM((TILE, 2, 128), BF16),
            pltpu.VMEM((256, TILE), BF16),
            pltpu.VMEM((4, 272, 256), F32),
            pltpu.VMEM((ROWS, 24, 128), F32),
            pltpu.VMEM((ROWS, 24, 128), F32),
            pltpu.VMEM((ROWS, 16, 128), F32),
            pltpu.VMEM((16, 128), F32),
            pltpu.VMEM((16, 128), BF16),
            pltpu.VMEM((ROWS, 16, 128), BF16),
            pltpu.VMEM((SUBS, ROWS, 16, 128), BF16),
            pltpu.VMEM((16, 2, 16, 128), F32),
            pltpu.VMEM((SUBS, 2, 8, TILE * TILES), I32),
            pltpu.VMEM((256, TILE * TILES), BF16),
            pltpu.VMEM((2, TILE, 256), BF16),
            pltpu.VMEM((256, 256), F32),
            pltpu.VMEM((8, SUBS, 32, 256), BF16),
            pltpu.VMEM((ROWS, 32, 256), BF16),
            dma((2,)), dma((6,)), dma((6,)),
            dma((6,)), dma((2,)), dma((120,)), dma((2,)),
            dma((2,)), dma((2,)), dma((40,)), dma((2,)),
            dma((1,)), dma((SUBS,)),
            dma((1,)), dma((1,)), dma((1,)), dma((1,)), dma((1,)), dma((1,)),
            dma((1,)), dma((SUBS,)),
            dma((1,)), dma((1,)),
            dma((2,)),
        ],
        compiler_params=pltpu.CompilerParams(
            collective_id=1, has_side_effects=True, vmem_limit_bytes=56 * MIB
        ),
        cost_estimate=pl.CostEstimate(
            flops=20 * 10**9, bytes_accessed=40 * 10**6, transcendentals=0
        ),
        name="step",
    )(ids, vectors, centroids, rotation, codes)


def local(vectors, list_ids, centroids, rotation, codes):
    sub = lax.axis_index("sub")
    owner, inner = list_ids // 128, list_ids % 128
    at_row, at_sub = owner // 4, owner % 4
    apart = (at_sub - sub + 4) % 4
    near = jnp.where(apart < 2, apart, 5 - apart)
    at_y, at_z, at_core = at_row // 8, (at_row // 2) % 4, at_row % 2
    half = inner // 64
    block = jnp.where(half == 0, at_z * 4 + at_y, at_y * 4 + at_z)
    ids = (((at_core * 2 + half) * 16 + block) * 4 + near) * 64 + inner % 64
    books, cross_cov = step_call(
        ids, vectors, centroids, rotation, codes.reshape(2, 8, -1)
    )
    return books.transpose(0, 2, 1), cross_cov


def solution(mesh):
    placed = (
        P("rows", None),
        P("rows"),
        P(("rows", "sub"), None),
        P(None, "sub"),
        P("sub", "rows"),
    )
    return jax.shard_map(
        local,
        mesh=mesh,
        in_specs=placed,
        out_specs=(P("sub", None, None), P("rows", "sub")),
        check_vma=False,
    )
```

```python
import jax
import jax.numpy as jnp
from jax import lax
from jax.experimental import pallas as pl
from jax.experimental.pallas import tpu as pltpu
from jax.sharding import PartitionSpec as P

KS = 256
MIB = 2**20
MESH = pl.DeviceIdType.MESH
ROWS, SUBS = 32, 4
TILE, TILES = 1024, 8
ROUNDS = ((0, 1), (1, 3), (3, 4))
F32, BF16, I32 = jnp.float32, jnp.bfloat16, jnp.int32
TABLE = (2, 2, 4, 4, 4, 64, 2, 128)


def nt(a, b):
    return lax.dot_general(a, b, (((1,), (1,)), ((), ())), preferred_element_type=F32)


def step_kernel(
    ids, v, c, rot, codes, outbooks, cross,
    tab1, tab2, near, stage1, stage2, vbuf, vr, got, turned, acc, part, partgot, means,
    chunk, bchunk, rounded, every, books, diagonal, every_codes, resid, vcol, total, piece, piecegot,
    vsem, xs, xr, l1, s1, r1, o1, l2, s2, r2, o2, cs, cr, ps, pr, ms, mr, bs, br, ys, yr, ws, wr,
    vcsem,
):
    row = lax.axis_index("rows")
    sub = lax.axis_index("sub")
    core = lax.rem(row, 2)
    z = lax.rem(row // 2, 4)
    y = row // 8
    block = row // 8

    def up(i):
        return lax.rem(i + 1, 4)

    def down(i):
        return lax.rem(i + 3, 4)

    def device(at_y, at_z):
        return ((at_y * 4 + at_z) * 2 + core, sub)

    beside = (row + 1 - 2 * core, sub)
    after = ((device(up(y), z), device(down(y), z)), (device(y, up(z)), device(y, down(z))))
    across = ((row, up(sub)), (row, down(sub)))

    barrier = pltpu.get_barrier_semaphore()
    for peer in after[0] + after[1] + across + (beside,):
        pl.semaphore_signal(barrier, inc=1, device_id=peer, device_id_type=MESH)

    def remote(src, dst, send, recv, to):
        return pltpu.make_async_remote_copy(
            src_ref=src, dst_ref=dst, send_sem=send, recv_sem=recv,
            device_id=to, device_id_type=MESH,
        )

    def v_copy(i):
        return pltpu.make_async_copy(
            v.at[pl.ds(i * TILE, TILE)], vbuf.at[lax.rem(i, 2)], vsem.at[lax.rem(i, 2)]
        )

    def turn_rows(first, last):
        def body(i, carry):
            v_copy(i).wait()

            @pl.when(i + 1 < TILES)
            def _():
                v_copy(i + 1).start()

            for h in range(2):
                value = jnp.dot(
                    vbuf[lax.rem(i, 2), h * 512:(h + 1) * 512, :], rot[...],
                    preferred_element_type=F32,
                )
                vr[pl.ds(pl.multiple_of(i * TILE + h * 512, 512), 512), :] = value
            return carry

        lax.fori_loop(first, last, body, 0)

    v_copy(0).start()
    turn_rows(0, 3)
    pl.semaphore_wait(barrier, 7)

    def exchange(k):
        half = pl.ds((0, 64, 64, 0, 0, 64)[k], 64)
        from_up = k % 2
        if k < 4:
            src, dst = c.at[half], near.at[1 - from_up, half]
        else:
            src, dst = near.at[1 - from_up, half], near.at[2, half]
        return remote(src, dst, xs.at[k], xr.at[k], across[from_up])

    class Gather:
        def __init__(self, table, stage, rounds, lsem, ssem, rsem, osem):
            self.table, self.stage, self.rounds = table, stage, rounds
            self.lsem, self.ssem, self.rsem, self.osem = lsem, ssem, rsem, osem

        def place(self, rnd, h):
            first, last = self.rounds[rnd]
            u, w = (y, z) if h == 0 else (z, y)
            return pl.ds(first, last - first), u, w

        def hop(self, rnd, h, phase, k, j=0):
            qs, u, w = self.place(rnd, h)
            to = after[h if phase == 0 else 1 - h][k % 2]
            mine = self.table.at[core, h]
            half = pl.ds(0, 32) if k == 2 else pl.ds(32, 32)
            if phase == 0:
                if k < 2:
                    src, dst = self.stage.at[qs, h], mine.at[w, u, qs]
                else:
                    src = dst = mine.at[w, down(u) if k == 2 else up(u), qs, half]
            else:
                at = (u, down(u), up(u), lax.rem(u + 2, 4))[j]
                if k < 2:
                    src, dst = mine.at[w, at, qs], mine.at[w, at, qs]
                    if j == 0:
                        src = self.stage.at[qs, h]
                else:
                    src = dst = mine.at[down(w) if k == 2 else up(w), at, qs, half]
            number = (rnd * 2 + h) * 20 + (k if phase == 0 else 4 + 4 * j + k)
            return remote(src, dst, self.ssem.at[phase], self.rsem.at[number], to)

        def keep(self, rnd, h):
            qs, u, w = self.place(rnd, h)
            return pltpu.make_async_copy(
                self.stage.at[qs, h], self.table.at[core, h, w, u, qs], self.lsem.at[rnd * 2 + h]
            )

        def over(self, rnd, h, j):
            qs, u, w = self.place(rnd, h)
            w = (w, down(w), up(w), lax.rem(w + 2, 4))[j]
            blocks = self.table.at[core, h, w, :, qs]
            remote(blocks, blocks, self.osem.at[0], self.osem.at[1], beside).start()

        def begin(self, rnd):
            for h in range(2):
                self.keep(rnd, h).start()
            for h in range(2):
                for k in range(2):
                    self.hop(rnd, h, 0, k).start()
            for h in range(2):
                for k in range(2):
                    self.hop(rnd, h, 1, k).start()

        def sides(self, rnd):
            for k in range(2):
                for h in range(2):
                    self.hop(rnd, h, 0, k).wait_recv()
                    self.hop(rnd, h, 0, k + 2).start()
            for j in (1, 2):
                for h in range(2):
                    for k in range(2):
                        self.hop(rnd, h, 1, k, j).start()

        def opposite(self, rnd):
            for h in range(2):
                for k in (2, 3):
                    self.hop(rnd, h, 0, k).wait_recv()
                for k in range(2):
                    self.hop(rnd, h, 1, k, 3).start()
            for h in range(2):
                self.keep(rnd, h).wait()
                self.over(rnd, h, 0)

        def forward(self, rnd, *blocks):
            for j in blocks:
                for k in range(2):
                    for h in range(2):
                        self.hop(rnd, h, 1, k, j).wait_recv()
                        self.hop(rnd, h, 1, k + 2, j).start()
            if blocks[-1] == 3:
                for h in range(2):
                    self.over(rnd, h, 1)
                    self.over(rnd, h, 2)

        def finish(self, rnd):
            for h in range(2):
                for j in range(4):
                    for k in (2, 3):
                        self.hop(rnd, h, 1, k, j).wait_recv()
                self.over(rnd, h, 3)

        def all_of(self, blocks, sem):
            pltpu.make_async_copy(blocks, blocks, sem).wait()

        def have(self):
            self.all_of(self.table.at[0], self.osem.at[1])

        def drain(self):
            self.all_of(self.table.at[0, :, 0, pl.ds(0, 3)], self.ssem.at[0])
            self.all_of(self.table.at[0, :, pl.ds(0, 3)], self.ssem.at[1])
            self.all_of(self.table.at[0], self.osem.at[0])

    first_table = Gather(tab1, stage1, ROUNDS, l1, s1, r1, o1)
    second_table = Gather(tab2, stage2, ((0, 4),), l2, s2, r2, o2)
    first_column = pl.multiple_of(sub * 256, 256)

    def project(q, at):
        value = jnp.dot(at[...], rot[...], preferred_element_type=F32)
        stage1[q] = value.astype(BF16).reshape(2, 64, 2, 128)

    def columns(q, at):
        stage2[q] = at[:, pl.ds(first_column, 256)].reshape(2, 64, 2, 128)

    def share_codes(p):
        return remote(
            codes, every_codes.at[sub], cs.at[0], cr.at[sub], (row, lax.rem(sub + p, SUBS))
        )

    def shared_codes(p):
        source = lax.rem(sub + p, SUBS)
        return remote(codes, every_codes.at[source], cs.at[0], cr.at[source], (row, source))

    for k in range(4):
        exchange(k).start()
    project(0, c)
    first_table.begin(0)
    own_codes = pltpu.make_async_copy(codes, every_codes.at[sub], cr.at[sub])
    own_codes.start()
    columns(0, c)
    first_table.sides(0)
    first_table.opposite(0)
    for k in range(2):
        exchange(k).wait_recv()
        exchange(k + 4).start()
    turn_rows(3, 5)
    first_table.forward(0, 0)
    exchange(2).wait_recv()
    exchange(3).wait_recv()
    project(1, near.at[0])
    project(2, near.at[1])
    first_table.begin(1)
    first_table.forward(0, 1, 2)
    turn_rows(5, 6)
    exchange(4).wait_recv()
    exchange(5).wait_recv()
    project(3, near.at[2])
    first_table.begin(2)
    first_table.sides(1)
    first_table.sides(2)
    first_table.forward(0, 3)
    turn_rows(6, 7)
    first_table.opposite(1)
    first_table.opposite(2)
    for p in range(1, SUBS):
        share_codes(p).start()
    turn_rows(7, 8)
    first_table.forward(1, 0)
    first_table.forward(2, 0)
    first_table.forward(1, 1, 2)
    first_table.forward(2, 1, 2)
    first_table.forward(1, 3)
    first_table.forward(2, 3)
    for q in range(3):
        columns(q + 1, near.at[q])
    second_table.begin(0)
    acc[...] = jnp.zeros_like(acc)
    for rnd in range(3):
        first_table.finish(rnd)
    second_table.sides(0)
    first_table.have()

    def gather_rows(table, base, count, at):
        flat = table.reshape(16384, 2, 128)
        for s in range(0, count, 32):
            rows = [flat[ids[base + s + j]] for j in range(32)]
            for j in range(32):
                got[at + s + j] = rows[j]

    def gather_tile(table, i):
        def body(s, carry):
            gather_rows(table, i * TILE + s * 32, 32, s * 32)
            return carry

        lax.fori_loop(0, TILE // 32, body, 0)

    high = lax.broadcasted_iota(I32, (64, TILE), 0)
    low = lax.broadcasted_iota(I32, (4, TILE), 0)
    gather_tile(tab1, 0)

    def sum_tile(i, carry):
        @pl.when(i == 0)
        def _():
            second_table.opposite(0)

        @pl.when(i == 2)
        def _():
            second_table.forward(0, 0)

        @pl.when(i == 3)
        def _():
            second_table.forward(0, 1)

        @pl.when(i == 4)
        def _():
            second_table.forward(0, 2)

        @pl.when(i == 6)
        def _():
            second_table.forward(0, 3)

        at = pl.multiple_of(i * TILE, TILE)
        fetched = got[...].reshape(TILE, 256).astype(F32)
        rotated = vr[pl.ds(at, TILE), :] - fetched
        for h in range(2):
            turned[h * 128:(h + 1) * 128, :] = rotated[:, h * 128:(h + 1) * 128].T.astype(BF16)
        ahead = jnp.minimum(i + 1, TILES - 1) * TILE
        for grp in range(4):
            a, b, n = [], [], []
            for m in range(4 * grp, 4 * grp + 4):
                code = codes[m // 8, m % 8:m % 8 + 1, pl.ds(at, TILE)]
                a.append((high == (code & 63)).astype(BF16))
                mine = (low == (code >> 6)).astype(BF16)
                for l in range(4):
                    b.append(turned[m * 16:(m + 1) * 16, :] * mine[l:l + 1, :])
                n.append(mine)
            acc[grp] += nt(jnp.concatenate(b + n, axis=0), jnp.concatenate(a, axis=0))
            gather_rows(tab1, ahead + grp * 256, 256, grp * 256)
        return carry

    lax.fori_loop(0, TILES, sum_tile, 0)
    lane = lax.broadcasted_iota(I32, (1, 128), 1)
    for grp in range(4):
        for pair in range(2):
            cols = slice(pair * 128, pair * 128 + 128)
            m = 2 * pair
            both = jnp.where(
                lane < 64, acc[grp, m * 64:(m + 1) * 64, cols],
                acc[grp, (m + 1) * 64:(m + 2) * 64, cols],
            )
            count = jnp.where(
                lane < 64, acc[grp, 256 + m * 4:256 + m * 4 + 4, cols],
                acc[grp, 256 + m * 4 + 4:256 + m * 4 + 8, cols],
            )
            for l in range(4):
                at = (2 * grp + pair) * 4 + l
                part[at, :16, :] = both[l * 16:(l + 1) * 16, :]
                part[at, 16:17, :] = count[l:l + 1, :]

    def each(f, first=1):
        def body(p, carry):
            f(p)
            return carry

        lax.fori_loop(first, ROWS, body, 0)

    def scatter(p):
        to = lax.rem(row + p, ROWS)
        remote(
            part.at[to, pl.ds(0, 17)], partgot.at[row, pl.ds(0, 17)], ps.at[0], pr.at[0], (to, sub)
        ).start()

    def give(p):
        to = lax.rem(row + p, ROWS)
        remote(bchunk, rounded.at[row], bs.at[0], br.at[0], (to, sub)).start()

    def publish(p):
        to = lax.rem(row + p, ROWS)
        remote(chunk, means.at[row], ms.at[0], mr.at[0], (to, sub)).start()

    def all_of(blocks, sem):
        pltpu.make_async_copy(blocks, blocks, sem).wait()

    others = pl.ds(0, ROWS - 1)

    def spread_books(p):
        to = (row, lax.rem(sub + p, SUBS))
        return remote(rounded, every.at[sub], ys.at[0], yr.at[sub], to)

    def spread_got(p):
        source = lax.rem(sub + p, SUBS)
        return remote(rounded, every.at[source], ys.at[0], yr.at[source], (row, source))

    def column_copy(i):
        return pltpu.make_async_copy(
            v.at[pl.ds(i * TILE, TILE), pl.ds(first_column, 256)],
            vcol.at[lax.rem(i, 2)], vcsem.at[lax.rem(i, 2)],
        )

    each(scatter)
    column_copy(0).start()
    partgot[row] = part[row]
    second_table.finish(0)
    first_table.drain()
    all_of(partgot.at[others, pl.ds(0, 17)], pr.at[0])
    value = jnp.sum(partgot[:, :17, :], axis=0)
    mean = value[:16, :] / value[16:17, :]
    chunk[...] = mean
    bchunk[...] = mean.astype(BF16)
    means[row] = mean
    rounded[row] = mean.astype(BF16)
    each(give)
    each(publish)
    second_table.have()
    gather_tile(tab2, 0)
    all_of(rounded.at[others], br.at[0])
    every[sub] = rounded[...]
    for p in range(1, SUBS):
        spread_books(p).start()
    own_codes.wait()

    def send_piece(p, r):
        s = lax.rem(sub + p, SUBS)
        return remote(
            piece.at[r, p], piecegot.at[row], ws.at[0], wr.at[0], (sub * 8 + r, s)
        )

    def to_me(p, r):
        return jnp.logical_and(sub * 8 + r == row, p == 0)

    for p in range(SUBS):
        s = lax.rem(sub + p, SUBS)
        if p:
            spread_got(p).wait_recv()
            shared_codes(p).wait_recv()

        for q in range(6):
            for half in range(2):
                left = every[s, q * 4 + 2 * half].astype(F32)
                right = every[s, q * 4 + 2 * half + 1].astype(F32)
                books[2 * q, half] = jnp.where(lane < 64, left, pltpu.roll(right, 64, 1))
                books[2 * q + 1, half] = jnp.where(lane < 64, pltpu.roll(left, 64, 1), right)
        for q in range(2):
            for l in range(4):
                pair = every[s, 24 + q * 4 + l].astype(F32)
                rows = slice(l * 16, l * 16 + 16)
                diagonal[q, rows, :] = jnp.where(lane < 64, pair, 0.0).astype(BF16)
                rows = slice(64 + l * 16, 64 + l * 16 + 16)
                diagonal[q, rows, :] = jnp.where(lane < 64, 0.0, pair).astype(BF16)
        total[...] = jnp.zeros_like(total)

        def cross_tile(i, carry):
            if p == 0:
                column_copy(i).wait()

                @pl.when(i + 1 < TILES)
                def _():
                    column_copy(i + 1).start()

                fetched = got[...].reshape(TILE, 256).astype(F32)
                value = vcol[lax.rem(i, 2)].astype(F32) - fetched
                resid[pl.ds(pl.multiple_of(i * TILE, TILE), TILE), :] = value.astype(BF16)
                ahead = jnp.minimum(i + 1, TILES - 1) * TILE

            for quarter in range(TILE // 256):
                built = []
                at = pl.multiple_of(i * TILE + quarter * 256, 256)
                for m in range(12):
                    pieces = []
                    for t in range(2):
                        cols = pl.ds(pl.multiple_of(at + t * 128, 128), 128)
                        code = jnp.broadcast_to(every_codes[s, m // 8, m % 8:m % 8 + 1, cols], (8, 128))
                        inner = code & 127
                        both = []
                        for d in range(2):
                            low_half = books[m, 0, d * 8:(d + 1) * 8, :]
                            high_half = books[m, 1, d * 8:(d + 1) * 8, :]
                            both.append(jnp.where(
                                code >= 128,
                                jnp.take_along_axis(high_half, inner, axis=1),
                                jnp.take_along_axis(low_half, inner, axis=1),
                            ))
                        pieces.append(jnp.concatenate(both, axis=0).astype(BF16))
                    built.append(jnp.concatenate(pieces, axis=1))
                for g in range(2):
                    code = [
                        every_codes[s, 1, 4 + g * 2 + m:5 + g * 2 + m, pl.ds(at, 256)] for m in range(2)
                    ]
                    hot = [(high[:, :256] == (code[m] & 63)).astype(BF16) for m in range(2)]
                    picked = jnp.dot(
                        diagonal[g], jnp.concatenate(hot, axis=0), preferred_element_type=F32
                    )
                    for m in range(2):
                        value = picked[m * 64:m * 64 + 16, :]
                        for l in range(1, 4):
                            other = picked[m * 64 + l * 16:m * 64 + (l + 1) * 16, :]
                            value = jnp.where(code[m] >= l * 64, other, value)
                        built.append(value.astype(BF16))
                total[...] += jnp.dot(
                    jnp.concatenate(built, axis=0), resid[pl.ds(at, 256), :],
                    preferred_element_type=F32,
                )
                if p == 0:
                    gather_rows(tab2, ahead + quarter * 256, 256, quarter * 256)
            return carry

        lax.fori_loop(0, TILES, cross_tile, 0)
        value = (total[...] * (1.0 / KS)).T.astype(BF16)
        for r in range(8):
            piece[r, p] = value[r * 32:(r + 1) * 32, :]
        for r in range(8):
            if p:
                send_piece(p, r).start()
            else:
                @pl.when(to_me(p, r))
                def _():
                    pltpu.make_async_copy(piece.at[r, p], piecegot.at[row], wr.at[0]).start()

                @pl.when(jnp.logical_not(to_me(p, r)))
                def _():
                    send_piece(p, r).start()

    for k in range(6):
        exchange(k).wait_send()
    second_table.drain()
    all_of(every_codes.at[pl.ds(0, SUBS - 1)], cs.at[0])
    all_of(every.at[pl.ds(0, SUBS - 1)], ys.at[0])
    all_of(partgot.at[others, pl.ds(0, 17)], ps.at[0])
    all_of(rounded.at[others], bs.at[0])
    all_of(means.at[others], ms.at[0])
    all_of(means.at[others], mr.at[0])

    for q in range(8):
        for half in range(2):
            left, right = means[q * 4 + 2 * half], means[q * 4 + 2 * half + 1]
            cols = slice(half * 128, half * 128 + 128)
            outbooks[2 * q, :, cols] = jnp.where(lane < 64, left, pltpu.roll(right, 64, 1))
            outbooks[2 * q + 1, :, cols] = jnp.where(lane < 64, pltpu.roll(left, 64, 1), right)
    all_of(piecegot, wr.at[0])
    value = jnp.zeros(cross.shape, F32)
    for r in range(ROWS):
        value = value + piecegot[r].astype(F32)
    cross[...] = value

    @pl.when(sub == block)
    def _():
        all_of(piecegot.at[others], ws.at[0])

    @pl.when(sub != block)
    def _():
        all_of(piecegot, ws.at[0])


def step_call(ids, vectors, centroids, rotation, codes):
    vmem = pl.BlockSpec(memory_space=pltpu.VMEM)
    dma = pltpu.SemaphoreType.DMA
    return pl.pallas_call(
        step_kernel,
        out_shape=(
            jax.ShapeDtypeStruct((16, 16, 256), F32),
            jax.ShapeDtypeStruct((32, 256), F32),
        ),
        in_specs=[
            pl.BlockSpec(memory_space=pltpu.SMEM),
            pl.BlockSpec(memory_space=pl.ANY),
            vmem, vmem, vmem,
        ],
        out_specs=(vmem, vmem),
        scratch_shapes=[
            pltpu.VMEM(TABLE, BF16),
            pltpu.VMEM(TABLE, BF16),
            pltpu.VMEM((3, 128, 1024), BF16),
            pltpu.VMEM((4, 2, 64, 2, 128), BF16),
            pltpu.VMEM((4, 2, 64, 2, 128), BF16),
            pltpu.VMEM((2, TILE, 1024), BF16),
            pltpu.VMEM((TILE * TILES, 256), F32),
            pltpu.VMEM((TILE, 2, 128), BF16),
            pltpu.VMEM((256, TILE), BF16),
            pltpu.VMEM((4, 272, 256), F32),
            pltpu.VMEM((ROWS, 24, 128), F32),
            pltpu.VMEM((ROWS, 24, 128), F32),
            pltpu.VMEM((ROWS, 16, 128), F32),
            pltpu.VMEM((16, 128), F32),
            pltpu.VMEM((16, 128), BF16),
            pltpu.VMEM((ROWS, 16, 128), BF16),
            pltpu.VMEM((SUBS, ROWS, 16, 128), BF16),
            pltpu.VMEM((12, 2, 16, 128), F32),
            pltpu.VMEM((2, 128, 128), BF16),
            pltpu.VMEM((SUBS, 2, 8, TILE * TILES), I32),
            pltpu.VMEM((TILE * TILES, 256), BF16),
            pltpu.VMEM((2, TILE, 256), BF16),
            pltpu.VMEM((256, 256), F32),
            pltpu.VMEM((8, SUBS, 32, 256), BF16),
            pltpu.VMEM((ROWS, 32, 256), BF16),
            dma((2,)), dma((6,)), dma((6,)),
            dma((6,)), dma((2,)), dma((120,)), dma((2,)),
            dma((2,)), dma((2,)), dma((40,)), dma((2,)),
            dma((1,)), dma((SUBS,)),
            dma((1,)), dma((1,)), dma((1,)), dma((1,)), dma((1,)), dma((1,)),
            dma((1,)), dma((SUBS,)),
            dma((1,)), dma((1,)),
            dma((2,)),
        ],
        compiler_params=pltpu.CompilerParams(
            collective_id=1, has_side_effects=True, vmem_limit_bytes=56 * MIB
        ),
        cost_estimate=pl.CostEstimate(
            flops=20 * 10**9, bytes_accessed=40 * 10**6, transcendentals=0
        ),
        name="step",
    )(ids, vectors, centroids, rotation, codes)


def local(vectors, list_ids, centroids, rotation, codes):
    sub = lax.axis_index("sub")
    owner, inner = list_ids // 128, list_ids % 128
    at_row, at_sub = owner // 4, owner % 4
    apart = (at_sub - sub + 4) % 4
    near = jnp.where(apart < 2, apart, 5 - apart)
    at_y, at_z, at_core = at_row // 8, (at_row // 2) % 4, at_row % 2
    half = inner // 64
    block = jnp.where(half == 0, at_z * 4 + at_y, at_y * 4 + at_z)
    ids = (((at_core * 2 + half) * 16 + block) * 4 + near) * 64 + inner % 64
    books, cross_cov = step_call(
        ids, vectors, centroids, rotation, codes.reshape(2, 8, -1)
    )
    return books.transpose(0, 2, 1), cross_cov


def solution(mesh):
    placed = (
        P("rows", None),
        P("rows"),
        P(("rows", "sub"), None),
        P(None, "sub"),
        P("sub", "rows"),
    )
    return jax.shard_map(
        local,
        mesh=mesh,
        in_specs=placed,
        out_specs=(P("sub", None, None), P("rows", "sub")),
        check_vma=False,
    )
```

```python
import jax
import jax.numpy as jnp
from jax import lax
from jax.experimental import pallas as pl
from jax.experimental.pallas import tpu as pltpu
from jax.sharding import PartitionSpec as P

KS = 256
MIB = 2**20
MESH = pl.DeviceIdType.MESH
ROWS, SUBS = 32, 4
TILE, TILES = 1024, 8
ROUNDS = ((0, 1), (1, 3), (3, 4))
F32, BF16, I32 = jnp.float32, jnp.bfloat16, jnp.int32
TABLE = (2, 2, 4, 4, 4, 64, 2, 128)


def nt(a, b):
    return lax.dot_general(a, b, (((1,), (1,)), ((), ())), preferred_element_type=F32)


def step_kernel(
    ids, v, c, rot, codes, outbooks, cross,
    tab1, tab2, near, stage1, stage2, vbuf, vr, got, turned, acc, part, partgot, means,
    chunk, bchunk, rounded, every, books, diagonal, every_codes, resid, vcol, total, piece, piecegot,
    vsem, xs, xr, l1, s1, r1, o1, l2, s2, r2, o2, cs, cr, ps, pr, ms, mr, bs, br, ys, yr, ws, wr,
    vcsem,
):
    row = lax.axis_index("rows")
    sub = lax.axis_index("sub")
    core = lax.rem(row, 2)
    z = lax.rem(row // 2, 4)
    y = row // 8
    block = row // 8

    def up(i):
        return lax.rem(i + 1, 4)

    def down(i):
        return lax.rem(i + 3, 4)

    def device(at_y, at_z):
        return ((at_y * 4 + at_z) * 2 + core, sub)

    beside = (row + 1 - 2 * core, sub)
    after = ((device(up(y), z), device(down(y), z)), (device(y, up(z)), device(y, down(z))))
    across = ((row, up(sub)), (row, down(sub)))

    barrier = pltpu.get_barrier_semaphore()
    for peer in after[0] + after[1] + across + (beside,):
        pl.semaphore_signal(barrier, inc=1, device_id=peer, device_id_type=MESH)

    def remote(src, dst, send, recv, to):
        return pltpu.make_async_remote_copy(
            src_ref=src, dst_ref=dst, send_sem=send, recv_sem=recv,
            device_id=to, device_id_type=MESH,
        )

    def v_copy(i):
        return pltpu.make_async_copy(
            v.at[pl.ds(i * TILE, TILE)], vbuf.at[lax.rem(i, 2)], vsem.at[lax.rem(i, 2)]
        )

    def turn_rows(first, last):
        def body(i, carry):
            v_copy(i).wait()

            @pl.when(i + 1 < TILES)
            def _():
                v_copy(i + 1).start()

            for h in range(2):
                value = jnp.dot(
                    vbuf[lax.rem(i, 2), h * 512:(h + 1) * 512, :], rot[...],
                    preferred_element_type=F32,
                )
                vr[pl.ds(pl.multiple_of(i * TILE + h * 512, 512), 512), :] = value
            return carry

        lax.fori_loop(first, last, body, 0)

    v_copy(0).start()
    turn_rows(0, 3)
    pl.semaphore_wait(barrier, 7)

    def exchange(k):
        half = pl.ds((0, 64, 64, 0, 0, 64)[k], 64)
        from_up = k % 2
        if k < 4:
            src, dst = c.at[half], near.at[1 - from_up, half]
        else:
            src, dst = near.at[1 - from_up, half], near.at[2, half]
        return remote(src, dst, xs.at[k], xr.at[k], across[from_up])

    class Gather:
        def __init__(self, table, stage, rounds, lsem, ssem, rsem, osem):
            self.table, self.stage, self.rounds = table, stage, rounds
            self.lsem, self.ssem, self.rsem, self.osem = lsem, ssem, rsem, osem

        def place(self, rnd, h):
            first, last = self.rounds[rnd]
            u, w = (y, z) if h == 0 else (z, y)
            return pl.ds(first, last - first), u, w

        def hop(self, rnd, h, phase, k, j=0):
            qs, u, w = self.place(rnd, h)
            to = after[h if phase == 0 else 1 - h][k % 2]
            mine = self.table.at[core, h]
            half = pl.ds(0, 32) if k == 2 else pl.ds(32, 32)
            if phase == 0:
                if k < 2:
                    src, dst = self.stage.at[qs, h], mine.at[w, u, qs]
                else:
                    src = dst = mine.at[w, down(u) if k == 2 else up(u), qs, half]
            else:
                at = (u, down(u), up(u), lax.rem(u + 2, 4))[j]
                if k < 2:
                    src, dst = mine.at[w, at, qs], mine.at[w, at, qs]
                    if j == 0:
                        src = self.stage.at[qs, h]
                else:
                    src = dst = mine.at[down(w) if k == 2 else up(w), at, qs, half]
            number = (rnd * 2 + h) * 20 + (k if phase == 0 else 4 + 4 * j + k)
            return remote(src, dst, self.ssem.at[phase], self.rsem.at[number], to)

        def keep(self, rnd, h):
            qs, u, w = self.place(rnd, h)
            return pltpu.make_async_copy(
                self.stage.at[qs, h], self.table.at[core, h, w, u, qs], self.lsem.at[rnd * 2 + h]
            )

        def over(self, rnd, h, j):
            qs, u, w = self.place(rnd, h)
            w = (w, down(w), up(w), lax.rem(w + 2, 4))[j]
            blocks = self.table.at[core, h, w, :, qs]
            remote(blocks, blocks, self.osem.at[0], self.osem.at[1], beside).start()

        def begin(self, rnd):
            for h in range(2):
                self.keep(rnd, h).start()
            for h in range(2):
                for k in range(2):
                    self.hop(rnd, h, 0, k).start()
            for h in range(2):
                for k in range(2):
                    self.hop(rnd, h, 1, k).start()

        def sides(self, rnd):
            for k in range(2):
                for h in range(2):
                    self.hop(rnd, h, 0, k).wait_recv()
                    self.hop(rnd, h, 0, k + 2).start()
            for j in (1, 2):
                for h in range(2):
                    for k in range(2):
                        self.hop(rnd, h, 1, k, j).start()

        def opposite(self, rnd):
            for h in range(2):
                for k in (2, 3):
                    self.hop(rnd, h, 0, k).wait_recv()
                for k in range(2):
                    self.hop(rnd, h, 1, k, 3).start()
            for h in range(2):
                self.keep(rnd, h).wait()
                self.over(rnd, h, 0)

        def forward(self, rnd, *blocks):
            for j in blocks:
                for k in range(2):
                    for h in range(2):
                        self.hop(rnd, h, 1, k, j).wait_recv()
                        self.hop(rnd, h, 1, k + 2, j).start()
            if blocks[-1] == 3:
                for h in range(2):
                    self.over(rnd, h, 1)
                    self.over(rnd, h, 2)

        def finish(self, rnd):
            for h in range(2):
                for j in range(4):
                    for k in (2, 3):
                        self.hop(rnd, h, 1, k, j).wait_recv()
                self.over(rnd, h, 3)

        def all_of(self, blocks, sem):
            pltpu.make_async_copy(blocks, blocks, sem).wait()

        def have(self):
            self.all_of(self.table.at[0], self.osem.at[1])

        def drain(self):
            self.all_of(self.table.at[0, :, 0, pl.ds(0, 3)], self.ssem.at[0])
            self.all_of(self.table.at[0, :, pl.ds(0, 3)], self.ssem.at[1])
            self.all_of(self.table.at[0], self.osem.at[0])

    first_table = Gather(tab1, stage1, ROUNDS, l1, s1, r1, o1)
    second_table = Gather(tab2, stage2, ((0, 4),), l2, s2, r2, o2)
    first_column = pl.multiple_of(sub * 256, 256)

    def project(q, at):
        value = jnp.dot(at[...], rot[...], preferred_element_type=F32)
        stage1[q] = value.astype(BF16).reshape(2, 64, 2, 128)

    def columns(q, at):
        stage2[q] = at[:, pl.ds(first_column, 256)].reshape(2, 64, 2, 128)

    def share_codes(p):
        return remote(
            codes, every_codes.at[sub], cs.at[0], cr.at[sub], (row, lax.rem(sub + p, SUBS))
        )

    def shared_codes(p):
        source = lax.rem(sub + p, SUBS)
        return remote(codes, every_codes.at[source], cs.at[0], cr.at[source], (row, source))

    for k in range(4):
        exchange(k).start()
    project(0, c)
    first_table.begin(0)
    own_codes = pltpu.make_async_copy(codes, every_codes.at[sub], cr.at[sub])
    own_codes.start()
    columns(0, c)
    first_table.sides(0)
    first_table.opposite(0)
    for k in range(2):
        exchange(k).wait_recv()
        exchange(k + 4).start()
    turn_rows(3, 5)
    first_table.forward(0, 0)
    exchange(2).wait_recv()
    exchange(3).wait_recv()
    project(1, near.at[0])
    project(2, near.at[1])
    first_table.begin(1)
    first_table.forward(0, 1, 2)
    turn_rows(5, 6)
    exchange(4).wait_recv()
    exchange(5).wait_recv()
    project(3, near.at[2])
    first_table.begin(2)
    first_table.sides(1)
    first_table.sides(2)
    first_table.forward(0, 3)
    turn_rows(6, 7)
    first_table.opposite(1)
    first_table.opposite(2)
    for p in range(1, SUBS):
        share_codes(p).start()
    turn_rows(7, 8)
    first_table.forward(1, 0)
    first_table.forward(2, 0)
    first_table.forward(1, 1, 2)
    first_table.forward(2, 1, 2)
    first_table.forward(1, 3)
    first_table.forward(2, 3)
    for q in range(3):
        columns(q + 1, near.at[q])
    second_table.begin(0)
    acc[...] = jnp.zeros_like(acc)
    for rnd in range(3):
        first_table.finish(rnd)
    second_table.sides(0)
    first_table.have()

    def gather_rows(table, base, count, at):
        flat = table.reshape(16384, 2, 128)
        for s in range(0, count, 32):
            rows = [flat[ids[base + s + j]] for j in range(32)]
            for j in range(32):
                got[at + s + j] = rows[j]

    def gather_tile(table, i):
        def body(s, carry):
            gather_rows(table, i * TILE + s * 32, 32, s * 32)
            return carry

        lax.fori_loop(0, TILE // 32, body, 0)

    high = lax.broadcasted_iota(I32, (64, TILE), 0)
    low = lax.broadcasted_iota(I32, (4, TILE), 0)
    gather_tile(tab1, 0)

    def sum_tile(i, carry):
        @pl.when(i == 1)
        def _():
            second_table.opposite(0)

        @pl.when(i == 3)
        def _():
            second_table.forward(0, 0)

        @pl.when(i == 4)
        def _():
            second_table.forward(0, 1)

        @pl.when(i == 5)
        def _():
            second_table.forward(0, 2)

        @pl.when(i == 7)
        def _():
            second_table.forward(0, 3)

        at = pl.multiple_of(i * TILE, TILE)
        fetched = got[...].reshape(TILE, 256).astype(F32)
        rotated = vr[pl.ds(at, TILE), :] - fetched
        for h in range(2):
            turned[h * 128:(h + 1) * 128, :] = rotated[:, h * 128:(h + 1) * 128].T.astype(BF16)
        ahead = jnp.minimum(i + 1, TILES - 1) * TILE
        for grp in range(4):
            a, b, n = [], [], []
            for m in range(4 * grp, 4 * grp + 4):
                code = codes[m // 8, m % 8:m % 8 + 1, pl.ds(at, TILE)]
                a.append((high == (code & 63)).astype(BF16))
                mine = (low == (code >> 6)).astype(BF16)
                for l in range(4):
                    b.append(turned[m * 16:(m + 1) * 16, :] * mine[l:l + 1, :])
                n.append(mine)
            acc[grp] += nt(jnp.concatenate(b + n, axis=0), jnp.concatenate(a, axis=0))
            gather_rows(tab1, ahead + grp * 256, 256, grp * 256)
        return carry

    lax.fori_loop(0, TILES, sum_tile, 0)
    lane = lax.broadcasted_iota(I32, (1, 128), 1)
    for grp in range(4):
        for pair in range(2):
            cols = slice(pair * 128, pair * 128 + 128)
            m = 2 * pair
            both = jnp.where(
                lane < 64, acc[grp, m * 64:(m + 1) * 64, cols],
                acc[grp, (m + 1) * 64:(m + 2) * 64, cols],
            )
            count = jnp.where(
                lane < 64, acc[grp, 256 + m * 4:256 + m * 4 + 4, cols],
                acc[grp, 256 + m * 4 + 4:256 + m * 4 + 8, cols],
            )
            for l in range(4):
                at = (2 * grp + pair) * 4 + l
                part[at, :16, :] = both[l * 16:(l + 1) * 16, :]
                part[at, 16:17, :] = count[l:l + 1, :]

    def each(f, first=1):
        def body(p, carry):
            f(p)
            return carry

        lax.fori_loop(first, ROWS, body, 0)

    def scatter(p):
        to = lax.rem(row + p, ROWS)
        remote(
            part.at[to, pl.ds(0, 17)], partgot.at[row, pl.ds(0, 17)], ps.at[0], pr.at[0], (to, sub)
        ).start()

    def give(p):
        to = lax.rem(row + p, ROWS)
        remote(bchunk, rounded.at[row], bs.at[0], br.at[0], (to, sub)).start()

    def publish(p):
        to = lax.rem(row + p, ROWS)
        remote(chunk, means.at[row], ms.at[0], mr.at[0], (to, sub)).start()

    def all_of(blocks, sem):
        pltpu.make_async_copy(blocks, blocks, sem).wait()

    others = pl.ds(0, ROWS - 1)

    def spread_books(p):
        to = (row, lax.rem(sub + p, SUBS))
        return remote(rounded, every.at[sub], ys.at[0], yr.at[sub], to)

    def spread_got(p):
        source = lax.rem(sub + p, SUBS)
        return remote(rounded, every.at[source], ys.at[0], yr.at[source], (row, source))

    def column_copy(i):
        return pltpu.make_async_copy(
            v.at[pl.ds(i * TILE, TILE), pl.ds(first_column, 256)],
            vcol.at[lax.rem(i, 2)], vcsem.at[lax.rem(i, 2)],
        )

    each(scatter)
    column_copy(0).start()
    partgot[row] = part[row]
    first_table.drain()
    all_of(partgot.at[others, pl.ds(0, 17)], pr.at[0])
    second_table.finish(0)
    value = jnp.sum(partgot[:, :17, :], axis=0)
    mean = value[:16, :] / value[16:17, :]
    chunk[...] = mean
    bchunk[...] = mean.astype(BF16)
    means[row] = mean
    rounded[row] = mean.astype(BF16)
    each(give)
    each(publish)
    second_table.have()
    gather_tile(tab2, 0)
    all_of(rounded.at[others], br.at[0])
    every[sub] = rounded[...]
    for p in range(1, SUBS):
        spread_books(p).start()
    own_codes.wait()

    def send_piece(p, r):
        s = lax.rem(sub + p, SUBS)
        return remote(
            piece.at[r, p], piecegot.at[row], ws.at[0], wr.at[0], (sub * 8 + r, s)
        )

    def to_me(p, r):
        return jnp.logical_and(sub * 8 + r == row, p == 0)

    for p in range(SUBS):
        s = lax.rem(sub + p, SUBS)
        if p:
            spread_got(p).wait_recv()
            shared_codes(p).wait_recv()

        for q in range(6):
            for half in range(2):
                left = every[s, q * 4 + 2 * half].astype(F32)
                right = every[s, q * 4 + 2 * half + 1].astype(F32)
                books[2 * q, half] = jnp.where(lane < 64, left, pltpu.roll(right, 64, 1))
                books[2 * q + 1, half] = jnp.where(lane < 64, pltpu.roll(left, 64, 1), right)
        for q in range(2):
            for l in range(4):
                pair = every[s, 24 + q * 4 + l].astype(F32)
                rows = slice(l * 16, l * 16 + 16)
                diagonal[q, rows, :] = jnp.where(lane < 64, pair, 0.0).astype(BF16)
                rows = slice(64 + l * 16, 64 + l * 16 + 16)
                diagonal[q, rows, :] = jnp.where(lane < 64, 0.0, pair).astype(BF16)
        total[...] = jnp.zeros_like(total)

        def cross_tile(i, carry):
            if p == 0:
                column_copy(i).wait()

                @pl.when(i + 1 < TILES)
                def _():
                    column_copy(i + 1).start()

                fetched = got[...].reshape(TILE, 256).astype(F32)
                value = vcol[lax.rem(i, 2)].astype(F32) - fetched
                resid[pl.ds(pl.multiple_of(i * TILE, TILE), TILE), :] = value.astype(BF16)
                ahead = jnp.minimum(i + 1, TILES - 1) * TILE

            for quarter in range(TILE // 256):
                built = []
                at = pl.multiple_of(i * TILE + quarter * 256, 256)
                for m in range(12):
                    pieces = []
                    for t in range(2):
                        cols = pl.ds(pl.multiple_of(at + t * 128, 128), 128)
                        code = jnp.broadcast_to(every_codes[s, m // 8, m % 8:m % 8 + 1, cols], (8, 128))
                        inner = code & 127
                        both = []
                        for d in range(2):
                            low_half = books[m, 0, d * 8:(d + 1) * 8, :]
                            high_half = books[m, 1, d * 8:(d + 1) * 8, :]
                            both.append(jnp.where(
                                code >= 128,
                                jnp.take_along_axis(high_half, inner, axis=1),
                                jnp.take_along_axis(low_half, inner, axis=1),
                            ))
                        pieces.append(jnp.concatenate(both, axis=0).astype(BF16))
                    built.append(jnp.concatenate(pieces, axis=1))
                for g in range(2):
                    code = [
                        every_codes[s, 1, 4 + g * 2 + m:5 + g * 2 + m, pl.ds(at, 256)] for m in range(2)
                    ]
                    hot = [(high[:, :256] == (code[m] & 63)).astype(BF16) for m in range(2)]
                    picked = jnp.dot(
                        diagonal[g], jnp.concatenate(hot, axis=0), preferred_element_type=F32
                    )
                    for m in range(2):
                        value = picked[m * 64:m * 64 + 16, :]
                        for l in range(1, 4):
                            other = picked[m * 64 + l * 16:m * 64 + (l + 1) * 16, :]
                            value = jnp.where(code[m] >= l * 64, other, value)
                        built.append(value.astype(BF16))
                total[...] += jnp.dot(
                    jnp.concatenate(built, axis=0), resid[pl.ds(at, 256), :],
                    preferred_element_type=F32,
                )
                if p == 0:
                    gather_rows(tab2, ahead + quarter * 256, 256, quarter * 256)
            return carry

        lax.fori_loop(0, TILES, cross_tile, 0)
        value = (total[...] * (1.0 / KS)).T.astype(BF16)
        for r in range(8):
            piece[r, p] = value[r * 32:(r + 1) * 32, :]
        for r in range(8):
            if p:
                send_piece(p, r).start()
            else:
                @pl.when(to_me(p, r))
                def _():
                    pltpu.make_async_copy(piece.at[r, p], piecegot.at[row], wr.at[0]).start()

                @pl.when(jnp.logical_not(to_me(p, r)))
                def _():
                    send_piece(p, r).start()

    for k in range(6):
        exchange(k).wait_send()
    second_table.drain()
    all_of(every_codes.at[pl.ds(0, SUBS - 1)], cs.at[0])
    all_of(every.at[pl.ds(0, SUBS - 1)], ys.at[0])
    all_of(partgot.at[others, pl.ds(0, 17)], ps.at[0])
    all_of(rounded.at[others], bs.at[0])
    all_of(means.at[others], ms.at[0])
    all_of(means.at[others], mr.at[0])

    for q in range(8):
        for half in range(2):
            left, right = means[q * 4 + 2 * half], means[q * 4 + 2 * half + 1]
            cols = slice(half * 128, half * 128 + 128)
            outbooks[2 * q, :, cols] = jnp.where(lane < 64, left, pltpu.roll(right, 64, 1))
            outbooks[2 * q + 1, :, cols] = jnp.where(lane < 64, pltpu.roll(left, 64, 1), right)
    all_of(piecegot, wr.at[0])
    value = jnp.zeros(cross.shape, F32)
    for r in range(ROWS):
        value = value + piecegot[r].astype(F32)
    cross[...] = value

    @pl.when(sub == block)
    def _():
        all_of(piecegot.at[others], ws.at[0])

    @pl.when(sub != block)
    def _():
        all_of(piecegot, ws.at[0])


def step_call(ids, vectors, centroids, rotation, codes):
    vmem = pl.BlockSpec(memory_space=pltpu.VMEM)
    dma = pltpu.SemaphoreType.DMA
    return pl.pallas_call(
        step_kernel,
        out_shape=(
            jax.ShapeDtypeStruct((16, 16, 256), F32),
            jax.ShapeDtypeStruct((32, 256), F32),
        ),
        in_specs=[
            pl.BlockSpec(memory_space=pltpu.SMEM),
            pl.BlockSpec(memory_space=pl.ANY),
            vmem, vmem, vmem,
        ],
        out_specs=(vmem, vmem),
        scratch_shapes=[
            pltpu.VMEM(TABLE, BF16),
            pltpu.VMEM(TABLE, BF16),
            pltpu.VMEM((3, 128, 1024), BF16),
            pltpu.VMEM((4, 2, 64, 2, 128), BF16),
            pltpu.VMEM((4, 2, 64, 2, 128), BF16),
            pltpu.VMEM((2, TILE, 1024), BF16),
            pltpu.VMEM((TILE * TILES, 256), F32),
            pltpu.VMEM((TILE, 2, 128), BF16),
            pltpu.VMEM((256, TILE), BF16),
            pltpu.VMEM((4, 272, 256), F32),
            pltpu.VMEM((ROWS, 24, 128), F32),
            pltpu.VMEM((ROWS, 24, 128), F32),
            pltpu.VMEM((ROWS, 16, 128), F32),
            pltpu.VMEM((16, 128), F32),
            pltpu.VMEM((16, 128), BF16),
            pltpu.VMEM((ROWS, 16, 128), BF16),
            pltpu.VMEM((SUBS, ROWS, 16, 128), BF16),
            pltpu.VMEM((12, 2, 16, 128), F32),
            pltpu.VMEM((2, 128, 128), BF16),
            pltpu.VMEM((SUBS, 2, 8, TILE * TILES), I32),
            pltpu.VMEM((TILE * TILES, 256), BF16),
            pltpu.VMEM((2, TILE, 256), BF16),
            pltpu.VMEM((256, 256), F32),
            pltpu.VMEM((8, SUBS, 32, 256), BF16),
            pltpu.VMEM((ROWS, 32, 256), BF16),
            dma((2,)), dma((6,)), dma((6,)),
            dma((6,)), dma((2,)), dma((120,)), dma((2,)),
            dma((2,)), dma((2,)), dma((40,)), dma((2,)),
            dma((1,)), dma((SUBS,)),
            dma((1,)), dma((1,)), dma((1,)), dma((1,)), dma((1,)), dma((1,)),
            dma((1,)), dma((SUBS,)),
            dma((1,)), dma((1,)),
            dma((2,)),
        ],
        compiler_params=pltpu.CompilerParams(
            collective_id=1, has_side_effects=True, vmem_limit_bytes=56 * MIB
        ),
        cost_estimate=pl.CostEstimate(
            flops=20 * 10**9, bytes_accessed=40 * 10**6, transcendentals=0
        ),
        name="step",
    )(ids, vectors, centroids, rotation, codes)


def local(vectors, list_ids, centroids, rotation, codes):
    sub = lax.axis_index("sub")
    owner, inner = list_ids // 128, list_ids % 128
    at_row, at_sub = owner // 4, owner % 4
    apart = (at_sub - sub + 4) % 4
    near = jnp.where(apart < 2, apart, 5 - apart)
    at_y, at_z, at_core = at_row // 8, (at_row // 2) % 4, at_row % 2
    half = inner // 64
    block = jnp.where(half == 0, at_z * 4 + at_y, at_y * 4 + at_z)
    ids = (((at_core * 2 + half) * 16 + block) * 4 + near) * 64 + inner % 64
    books, cross_cov = step_call(
        ids, vectors, centroids, rotation, codes.reshape(2, 8, -1)
    )
    return books.transpose(0, 2, 1), cross_cov


def solution(mesh):
    placed = (
        P("rows", None),
        P("rows"),
        P(("rows", "sub"), None),
        P(None, "sub"),
        P("sub", "rows"),
    )
    return jax.shard_map(
        local,
        mesh=mesh,
        in_specs=placed,
        out_specs=(P("sub", None, None), P("rows", "sub")),
        check_vma=False,
    )
```

```python
import jax
import jax.numpy as jnp
from jax import lax
from jax.experimental import pallas as pl
from jax.experimental.pallas import tpu as pltpu
from jax.sharding import PartitionSpec as P

KS = 256
MIB = 2**20
MESH = pl.DeviceIdType.MESH
ROWS, SUBS = 32, 4
TILE, TILES = 1024, 8
ROUNDS = ((0, 1), (1, 3), (3, 4))
F32, BF16, I32 = jnp.float32, jnp.bfloat16, jnp.int32
TABLE = (2, 2, 4, 4, 4, 64, 2, 128)


def nt(a, b):
    return lax.dot_general(a, b, (((1,), (1,)), ((), ())), preferred_element_type=F32)


def step_kernel(
    ids, v, c, rot, codes, outbooks, cross,
    tab1, tab2, near, stage1, stage2, vbuf, vr, got, turned, acc, part, partgot, means,
    chunk, bchunk, rounded, every, books, diagonal, every_codes, resid, vcol, total, piece, piecegot,
    vsem, xs, xr, l1, s1, r1, o1, l2, s2, r2, o2, cs, cr, ps, pr, ms, mr, bs, br, ys, yr, ws, wr,
    vcsem,
):
    row = lax.axis_index("rows")
    sub = lax.axis_index("sub")
    core = lax.rem(row, 2)
    z = lax.rem(row // 2, 4)
    y = row // 8
    block = row // 8

    def up(i):
        return lax.rem(i + 1, 4)

    def down(i):
        return lax.rem(i + 3, 4)

    def device(at_y, at_z):
        return ((at_y * 4 + at_z) * 2 + core, sub)

    beside = (row + 1 - 2 * core, sub)
    after = ((device(up(y), z), device(down(y), z)), (device(y, up(z)), device(y, down(z))))
    across = ((row, up(sub)), (row, down(sub)))

    barrier = pltpu.get_barrier_semaphore()
    for peer in after[0] + after[1] + across + (beside,):
        pl.semaphore_signal(barrier, inc=1, device_id=peer, device_id_type=MESH)

    def remote(src, dst, send, recv, to):
        return pltpu.make_async_remote_copy(
            src_ref=src, dst_ref=dst, send_sem=send, recv_sem=recv,
            device_id=to, device_id_type=MESH,
        )

    def v_copy(i):
        return pltpu.make_async_copy(
            v.at[pl.ds(i * TILE, TILE)], vbuf.at[lax.rem(i, 2)], vsem.at[lax.rem(i, 2)]
        )

    def turn_rows(first, last):
        def body(i, carry):
            v_copy(i).wait()

            @pl.when(i + 1 < TILES)
            def _():
                v_copy(i + 1).start()

            for h in range(2):
                value = jnp.dot(
                    vbuf[lax.rem(i, 2), h * 512:(h + 1) * 512, :], rot[...],
                    preferred_element_type=F32,
                )
                vr[pl.ds(pl.multiple_of(i * TILE + h * 512, 512), 512), :] = value
            return carry

        lax.fori_loop(first, last, body, 0)

    v_copy(0).start()
    turn_rows(0, 3)
    pl.semaphore_wait(barrier, 7)

    def exchange(k):
        half = pl.ds((0, 64, 64, 0, 0, 64)[k], 64)
        from_up = k % 2
        if k < 4:
            src, dst = c.at[half], near.at[1 - from_up, half]
        else:
            src, dst = near.at[1 - from_up, half], near.at[2, half]
        return remote(src, dst, xs.at[k], xr.at[k], across[from_up])

    class Gather:
        def __init__(self, table, stage, rounds, lsem, ssem, rsem, osem):
            self.table, self.stage, self.rounds = table, stage, rounds
            self.lsem, self.ssem, self.rsem, self.osem = lsem, ssem, rsem, osem

        def place(self, rnd, h):
            first, last = self.rounds[rnd]
            u, w = (y, z) if h == 0 else (z, y)
            return pl.ds(first, last - first), u, w

        def hop(self, rnd, h, phase, k, j=0):
            qs, u, w = self.place(rnd, h)
            to = after[h if phase == 0 else 1 - h][k % 2]
            mine = self.table.at[core, h]
            half = pl.ds(0, 32) if k == 2 else pl.ds(32, 32)
            if phase == 0:
                if k < 2:
                    src, dst = self.stage.at[qs, h], mine.at[w, u, qs]
                else:
                    src = dst = mine.at[w, down(u) if k == 2 else up(u), qs, half]
            else:
                at = (u, down(u), up(u), lax.rem(u + 2, 4))[j]
                if k < 2:
                    src, dst = mine.at[w, at, qs], mine.at[w, at, qs]
                    if j == 0:
                        src = self.stage.at[qs, h]
                else:
                    src = dst = mine.at[down(w) if k == 2 else up(w), at, qs, half]
            number = (rnd * 2 + h) * 20 + (k if phase == 0 else 4 + 4 * j + k)
            return remote(src, dst, self.ssem.at[phase], self.rsem.at[number], to)

        def keep(self, rnd, h):
            qs, u, w = self.place(rnd, h)
            return pltpu.make_async_copy(
                self.stage.at[qs, h], self.table.at[core, h, w, u, qs], self.lsem.at[rnd * 2 + h]
            )

        def over(self, rnd, h, j):
            qs, u, w = self.place(rnd, h)
            w = (w, down(w), up(w), lax.rem(w + 2, 4))[j]
            blocks = self.table.at[core, h, w, :, qs]
            remote(blocks, blocks, self.osem.at[0], self.osem.at[1], beside).start()

        def begin(self, rnd):
            for h in range(2):
                self.keep(rnd, h).start()
            for h in range(2):
                for k in range(2):
                    self.hop(rnd, h, 0, k).start()
            for h in range(2):
                for k in range(2):
                    self.hop(rnd, h, 1, k).start()

        def sides(self, rnd):
            for k in range(2):
                for h in range(2):
                    self.hop(rnd, h, 0, k).wait_recv()
                    self.hop(rnd, h, 0, k + 2).start()
            for j in (1, 2):
                for h in range(2):
                    for k in range(2):
                        self.hop(rnd, h, 1, k, j).start()

        def opposite(self, rnd):
            for h in range(2):
                for k in (2, 3):
                    self.hop(rnd, h, 0, k).wait_recv()
                for k in range(2):
                    self.hop(rnd, h, 1, k, 3).start()
            for h in range(2):
                self.keep(rnd, h).wait()
                self.over(rnd, h, 0)

        def forward(self, rnd, *blocks):
            for j in blocks:
                for k in range(2):
                    for h in range(2):
                        self.hop(rnd, h, 1, k, j).wait_recv()
                        self.hop(rnd, h, 1, k + 2, j).start()
            if blocks[-1] == 3:
                for h in range(2):
                    self.over(rnd, h, 1)
                    self.over(rnd, h, 2)

        def finish(self, rnd):
            for h in range(2):
                for j in range(4):
                    for k in (2, 3):
                        self.hop(rnd, h, 1, k, j).wait_recv()
                self.over(rnd, h, 3)

        def all_of(self, blocks, sem):
            pltpu.make_async_copy(blocks, blocks, sem).wait()

        def have(self):
            self.all_of(self.table.at[0], self.osem.at[1])

        def drain(self):
            self.all_of(self.table.at[0, :, 0, pl.ds(0, 3)], self.ssem.at[0])
            self.all_of(self.table.at[0, :, pl.ds(0, 3)], self.ssem.at[1])
            self.all_of(self.table.at[0], self.osem.at[0])

    first_table = Gather(tab1, stage1, ROUNDS, l1, s1, r1, o1)
    second_table = Gather(tab2, stage2, ((0, 4),), l2, s2, r2, o2)
    first_column = pl.multiple_of(sub * 256, 256)

    def project(q, at):
        value = jnp.dot(at[...], rot[...], preferred_element_type=F32)
        stage1[q] = value.astype(BF16).reshape(2, 64, 2, 128)

    def columns(q, at):
        stage2[q] = at[:, pl.ds(first_column, 256)].reshape(2, 64, 2, 128)

    def share_codes(p):
        return remote(
            codes, every_codes.at[sub], cs.at[0], cr.at[sub], (row, lax.rem(sub + p, SUBS))
        )

    def shared_codes(p):
        source = lax.rem(sub + p, SUBS)
        return remote(codes, every_codes.at[source], cs.at[0], cr.at[source], (row, source))

    for k in range(4):
        exchange(k).start()
    project(0, c)
    first_table.begin(0)
    own_codes = pltpu.make_async_copy(codes, every_codes.at[sub], cr.at[sub])
    own_codes.start()
    columns(0, c)
    first_table.sides(0)
    first_table.opposite(0)
    for k in range(2):
        exchange(k).wait_recv()
        exchange(k + 4).start()
    turn_rows(3, 5)
    first_table.forward(0, 0)
    exchange(2).wait_recv()
    exchange(3).wait_recv()
    project(1, near.at[0])
    project(2, near.at[1])
    first_table.begin(1)
    first_table.forward(0, 1, 2)
    turn_rows(5, 6)
    exchange(4).wait_recv()
    exchange(5).wait_recv()
    project(3, near.at[2])
    first_table.begin(2)
    first_table.sides(1)
    first_table.sides(2)
    first_table.forward(0, 3)
    turn_rows(6, 7)
    first_table.opposite(1)
    first_table.opposite(2)
    for p in range(1, SUBS):
        share_codes(p).start()
    turn_rows(7, 8)
    first_table.forward(1, 0)
    first_table.forward(2, 0)
    first_table.forward(1, 1, 2)
    first_table.forward(2, 1, 2)
    first_table.forward(1, 3)
    first_table.forward(2, 3)
    for q in range(3):
        columns(q + 1, near.at[q])
    acc[...] = jnp.zeros_like(acc)
    for rnd in range(3):
        first_table.finish(rnd)
    second_table.begin(0)
    first_table.have()
    second_table.sides(0)

    def gather_rows(table, base, count, at):
        flat = table.reshape(16384, 2, 128)
        for s in range(0, count, 32):
            rows = [flat[ids[base + s + j]] for j in range(32)]
            for j in range(32):
                got[at + s + j] = rows[j]

    def gather_tile(table, i):
        def body(s, carry):
            gather_rows(table, i * TILE + s * 32, 32, s * 32)
            return carry

        lax.fori_loop(0, TILE // 32, body, 0)

    high = lax.broadcasted_iota(I32, (64, TILE), 0)
    low = lax.broadcasted_iota(I32, (4, TILE), 0)
    gather_tile(tab1, 0)

    def sum_tile(i, carry):
        @pl.when(i == 1)
        def _():
            second_table.opposite(0)

        @pl.when(i == 3)
        def _():
            second_table.forward(0, 0)

        @pl.when(i == 4)
        def _():
            second_table.forward(0, 1)

        @pl.when(i == 5)
        def _():
            second_table.forward(0, 2)

        @pl.when(i == 7)
        def _():
            second_table.forward(0, 3)

        at = pl.multiple_of(i * TILE, TILE)
        fetched = got[...].reshape(TILE, 256).astype(F32)
        rotated = vr[pl.ds(at, TILE), :] - fetched
        for h in range(2):
            turned[h * 128:(h + 1) * 128, :] = rotated[:, h * 128:(h + 1) * 128].T.astype(BF16)
        ahead = jnp.minimum(i + 1, TILES - 1) * TILE
        for grp in range(4):
            a, b, n = [], [], []
            for m in range(4 * grp, 4 * grp + 4):
                code = codes[m // 8, m % 8:m % 8 + 1, pl.ds(at, TILE)]
                a.append((high == (code & 63)).astype(BF16))
                mine = (low == (code >> 6)).astype(BF16)
                for l in range(4):
                    b.append(turned[m * 16:(m + 1) * 16, :] * mine[l:l + 1, :])
                n.append(mine)
            acc[grp] += nt(jnp.concatenate(b + n, axis=0), jnp.concatenate(a, axis=0))
            gather_rows(tab1, ahead + grp * 256, 256, grp * 256)
        return carry

    lax.fori_loop(0, TILES, sum_tile, 0)
    lane = lax.broadcasted_iota(I32, (1, 128), 1)
    for grp in range(4):
        for pair in range(2):
            cols = slice(pair * 128, pair * 128 + 128)
            m = 2 * pair
            both = jnp.where(
                lane < 64, acc[grp, m * 64:(m + 1) * 64, cols],
                acc[grp, (m + 1) * 64:(m + 2) * 64, cols],
            )
            count = jnp.where(
                lane < 64, acc[grp, 256 + m * 4:256 + m * 4 + 4, cols],
                acc[grp, 256 + m * 4 + 4:256 + m * 4 + 8, cols],
            )
            for l in range(4):
                at = (2 * grp + pair) * 4 + l
                part[at, :16, :] = both[l * 16:(l + 1) * 16, :]
                part[at, 16:17, :] = count[l:l + 1, :]

    def each(f, first=1):
        def body(p, carry):
            f(p)
            return carry

        lax.fori_loop(first, ROWS, body, 0)

    def scatter(p):
        to = lax.rem(row + p, ROWS)
        remote(
            part.at[to, pl.ds(0, 17)], partgot.at[row, pl.ds(0, 17)], ps.at[0], pr.at[0], (to, sub)
        ).start()

    def give(p):
        to = lax.rem(row + p, ROWS)
        remote(bchunk, rounded.at[row], bs.at[0], br.at[0], (to, sub)).start()

    def publish(p):
        to = lax.rem(row + p, ROWS)
        remote(chunk, means.at[row], ms.at[0], mr.at[0], (to, sub)).start()

    def all_of(blocks, sem):
        pltpu.make_async_copy(blocks, blocks, sem).wait()

    others = pl.ds(0, ROWS - 1)

    def spread_books(p):
        to = (row, lax.rem(sub + p, SUBS))
        return remote(rounded, every.at[sub], ys.at[0], yr.at[sub], to)

    def spread_got(p):
        source = lax.rem(sub + p, SUBS)
        return remote(rounded, every.at[source], ys.at[0], yr.at[source], (row, source))

    def column_copy(i):
        return pltpu.make_async_copy(
            v.at[pl.ds(i * TILE, TILE), pl.ds(first_column, 256)],
            vcol.at[lax.rem(i, 2)], vcsem.at[lax.rem(i, 2)],
        )

    each(scatter)
    column_copy(0).start()
    partgot[row] = part[row]
    first_table.drain()
    all_of(partgot.at[others, pl.ds(0, 17)], pr.at[0])
    second_table.finish(0)
    value = jnp.sum(partgot[:, :17, :], axis=0)
    mean = value[:16, :] / value[16:17, :]
    chunk[...] = mean
    bchunk[...] = mean.astype(BF16)
    means[row] = mean
    rounded[row] = mean.astype(BF16)
    each(give)
    each(publish)
    second_table.have()
    gather_tile(tab2, 0)
    all_of(rounded.at[others], br.at[0])
    every[sub] = rounded[...]
    for p in range(1, SUBS):
        spread_books(p).start()
    own_codes.wait()

    def send_piece(p, r):
        s = lax.rem(sub + p, SUBS)
        return remote(
            piece.at[r, p], piecegot.at[row], ws.at[0], wr.at[0], (sub * 8 + r, s)
        )

    def to_me(p, r):
        return jnp.logical_and(sub * 8 + r == row, p == 0)

    for p in range(SUBS):
        s = lax.rem(sub + p, SUBS)
        if p:
            spread_got(p).wait_recv()
            shared_codes(p).wait_recv()

        for q in range(6):
            for half in range(2):
                left = every[s, q * 4 + 2 * half].astype(F32)
                right = every[s, q * 4 + 2 * half + 1].astype(F32)
                books[2 * q, half] = jnp.where(lane < 64, left, pltpu.roll(right, 64, 1))
                books[2 * q + 1, half] = jnp.where(lane < 64, pltpu.roll(left, 64, 1), right)
        for q in range(2):
            for l in range(4):
                pair = every[s, 24 + q * 4 + l].astype(F32)
                rows = slice(l * 16, l * 16 + 16)
                diagonal[q, rows, :] = jnp.where(lane < 64, pair, 0.0).astype(BF16)
                rows = slice(64 + l * 16, 64 + l * 16 + 16)
                diagonal[q, rows, :] = jnp.where(lane < 64, 0.0, pair).astype(BF16)
        total[...] = jnp.zeros_like(total)

        def cross_tile(i, carry):
            if p == 0:
                column_copy(i).wait()

                @pl.when(i + 1 < TILES)
                def _():
                    column_copy(i + 1).start()

                fetched = got[...].reshape(TILE, 256).astype(F32)
                value = vcol[lax.rem(i, 2)].astype(F32) - fetched
                resid[pl.ds(pl.multiple_of(i * TILE, TILE), TILE), :] = value.astype(BF16)
                ahead = jnp.minimum(i + 1, TILES - 1) * TILE

            for quarter in range(TILE // 256):
                built = []
                at = pl.multiple_of(i * TILE + quarter * 256, 256)
                for m in range(12):
                    pieces = []
                    for t in range(2):
                        cols = pl.ds(pl.multiple_of(at + t * 128, 128), 128)
                        code = jnp.broadcast_to(every_codes[s, m // 8, m % 8:m % 8 + 1, cols], (8, 128))
                        inner = code & 127
                        both = []
                        for d in range(2):
                            low_half = books[m, 0, d * 8:(d + 1) * 8, :]
                            high_half = books[m, 1, d * 8:(d + 1) * 8, :]
                            both.append(jnp.where(
                                code >= 128,
                                jnp.take_along_axis(high_half, inner, axis=1),
                                jnp.take_along_axis(low_half, inner, axis=1),
                            ))
                        pieces.append(jnp.concatenate(both, axis=0).astype(BF16))
                    built.append(jnp.concatenate(pieces, axis=1))
                for g in range(2):
                    code = [
                        every_codes[s, 1, 4 + g * 2 + m:5 + g * 2 + m, pl.ds(at, 256)] for m in range(2)
                    ]
                    hot = [(high[:, :256] == (code[m] & 63)).astype(BF16) for m in range(2)]
                    picked = jnp.dot(
                        diagonal[g], jnp.concatenate(hot, axis=0), preferred_element_type=F32
                    )
                    for m in range(2):
                        value = picked[m * 64:m * 64 + 16, :]
                        for l in range(1, 4):
                            other = picked[m * 64 + l * 16:m * 64 + (l + 1) * 16, :]
                            value = jnp.where(code[m] >= l * 64, other, value)
                        built.append(value.astype(BF16))
                total[...] += jnp.dot(
                    jnp.concatenate(built, axis=0), resid[pl.ds(at, 256), :],
                    preferred_element_type=F32,
                )
                if p == 0:
                    gather_rows(tab2, ahead + quarter * 256, 256, quarter * 256)
            return carry

        lax.fori_loop(0, TILES, cross_tile, 0)
        value = (total[...] * (1.0 / KS)).T.astype(BF16)
        for r in range(8):
            piece[r, p] = value[r * 32:(r + 1) * 32, :]
        for r in range(8):
            if p:
                send_piece(p, r).start()
            else:
                @pl.when(to_me(p, r))
                def _():
                    pltpu.make_async_copy(piece.at[r, p], piecegot.at[row], wr.at[0]).start()

                @pl.when(jnp.logical_not(to_me(p, r)))
                def _():
                    send_piece(p, r).start()

    for k in range(6):
        exchange(k).wait_send()
    second_table.drain()
    all_of(every_codes.at[pl.ds(0, SUBS - 1)], cs.at[0])
    all_of(every.at[pl.ds(0, SUBS - 1)], ys.at[0])
    all_of(partgot.at[others, pl.ds(0, 17)], ps.at[0])
    all_of(rounded.at[others], bs.at[0])
    all_of(means.at[others], ms.at[0])
    all_of(means.at[others], mr.at[0])

    for q in range(8):
        for half in range(2):
            left, right = means[q * 4 + 2 * half], means[q * 4 + 2 * half + 1]
            cols = slice(half * 128, half * 128 + 128)
            outbooks[2 * q, :, cols] = jnp.where(lane < 64, left, pltpu.roll(right, 64, 1))
            outbooks[2 * q + 1, :, cols] = jnp.where(lane < 64, pltpu.roll(left, 64, 1), right)
    all_of(piecegot, wr.at[0])
    value = jnp.zeros(cross.shape, F32)
    for r in range(ROWS):
        value = value + piecegot[r].astype(F32)
    cross[...] = value

    @pl.when(sub == block)
    def _():
        all_of(piecegot.at[others], ws.at[0])

    @pl.when(sub != block)
    def _():
        all_of(piecegot, ws.at[0])


def step_call(ids, vectors, centroids, rotation, codes):
    vmem = pl.BlockSpec(memory_space=pltpu.VMEM)
    dma = pltpu.SemaphoreType.DMA
    return pl.pallas_call(
        step_kernel,
        out_shape=(
            jax.ShapeDtypeStruct((16, 16, 256), F32),
            jax.ShapeDtypeStruct((32, 256), F32),
        ),
        in_specs=[
            pl.BlockSpec(memory_space=pltpu.SMEM),
            pl.BlockSpec(memory_space=pl.ANY),
            vmem, vmem, vmem,
        ],
        out_specs=(vmem, vmem),
        scratch_shapes=[
            pltpu.VMEM(TABLE, BF16),
            pltpu.VMEM(TABLE, BF16),
            pltpu.VMEM((3, 128, 1024), BF16),
            pltpu.VMEM((4, 2, 64, 2, 128), BF16),
            pltpu.VMEM((4, 2, 64, 2, 128), BF16),
            pltpu.VMEM((2, TILE, 1024), BF16),
            pltpu.VMEM((TILE * TILES, 256), F32),
            pltpu.VMEM((TILE, 2, 128), BF16),
            pltpu.VMEM((256, TILE), BF16),
            pltpu.VMEM((4, 272, 256), F32),
            pltpu.VMEM((ROWS, 24, 128), F32),
            pltpu.VMEM((ROWS, 24, 128), F32),
            pltpu.VMEM((ROWS, 16, 128), F32),
            pltpu.VMEM((16, 128), F32),
            pltpu.VMEM((16, 128), BF16),
            pltpu.VMEM((ROWS, 16, 128), BF16),
            pltpu.VMEM((SUBS, ROWS, 16, 128), BF16),
            pltpu.VMEM((12, 2, 16, 128), F32),
            pltpu.VMEM((2, 128, 128), BF16),
            pltpu.VMEM((SUBS, 2, 8, TILE * TILES), I32),
            pltpu.VMEM((TILE * TILES, 256), BF16),
            pltpu.VMEM((2, TILE, 256), BF16),
            pltpu.VMEM((256, 256), F32),
            pltpu.VMEM((8, SUBS, 32, 256), BF16),
            pltpu.VMEM((ROWS, 32, 256), BF16),
            dma((2,)), dma((6,)), dma((6,)),
            dma((6,)), dma((2,)), dma((120,)), dma((2,)),
            dma((2,)), dma((2,)), dma((40,)), dma((2,)),
            dma((1,)), dma((SUBS,)),
            dma((1,)), dma((1,)), dma((1,)), dma((1,)), dma((1,)), dma((1,)),
            dma((1,)), dma((SUBS,)),
            dma((1,)), dma((1,)),
            dma((2,)),
        ],
        compiler_params=pltpu.CompilerParams(
            collective_id=1, has_side_effects=True, vmem_limit_bytes=56 * MIB
        ),
        cost_estimate=pl.CostEstimate(
            flops=20 * 10**9, bytes_accessed=40 * 10**6, transcendentals=0
        ),
        name="step",
    )(ids, vectors, centroids, rotation, codes)


def local(vectors, list_ids, centroids, rotation, codes):
    sub = lax.axis_index("sub")
    owner, inner = list_ids // 128, list_ids % 128
    at_row, at_sub = owner // 4, owner % 4
    apart = (at_sub - sub + 4) % 4
    near = jnp.where(apart < 2, apart, 5 - apart)
    at_y, at_z, at_core = at_row // 8, (at_row // 2) % 4, at_row % 2
    half = inner // 64
    block = jnp.where(half == 0, at_z * 4 + at_y, at_y * 4 + at_z)
    ids = (((at_core * 2 + half) * 16 + block) * 4 + near) * 64 + inner % 64
    books, cross_cov = step_call(
        ids, vectors, centroids, rotation, codes.reshape(2, 8, -1)
    )
    return books.transpose(0, 2, 1), cross_cov


def solution(mesh):
    placed = (
        P("rows", None),
        P("rows"),
        P(("rows", "sub"), None),
        P(None, "sub"),
        P("sub", "rows"),
    )
    return jax.shard_map(
        local,
        mesh=mesh,
        in_specs=placed,
        out_specs=(P("sub", None, None), P("rows", "sub")),
        check_vma=False,
    )
```
